512 devices in a mesh: slide: 8 (over x, core), grid: 64 (over y, z).
Axes of the slice: x: 4, y: 4, z: 16, core: 2. Of those that a mesh axis runs over, the one named last changes fastest.
Arguments:
- embeddings: bfloat16 [8, 8192, 512], P('slide', 'grid'), may hold values from -6 to 6
- visible: int32 [8, 2048], P('slide'), may hold values from 0 to 8191, as said below
- window_id: int32 [8, 8192], P('slide'), may hold values from 0 to 126, as said below
- output_gradient: bfloat16 [8, 8192, 512], P('slide', 'grid'), may hold values from -6 to 6
- mask_token: float32 [512], replicated, may hold values from -4 to 4
- enc_qkv: bfloat16 [512, 1536], replicated, may hold values from -2 to 2
- enc_out: bfloat16 [512, 512], replicated, may hold values from -0.25 to 0.25
- dec_qkv: bfloat16 [512, 1536], replicated, may hold values from -2 to 2
- decoder_projected: bfloat16 [512, 512], replicated, may hold values from -0.25 to 0.25
Outputs:
- grad_embeddings: bfloat16 [8, 8192, 512], P('slide', 'grid')
- grad_enc_out: float32 [512, 512], P('grid', 'slide')
- grad_dec_out: float32 [512, 512], P('grid', 'slide')
The draws below stay inside these ranges and needn't reach their ends.
Inputs may be any that keep to these rules, and one draw needn't show every extreme that they name: Each row holds 2048 different tile numbers in ascending order. Visible tiles come in aligned runs of 32; in every slide all 128 tiles of one block of 128 aligned tiles are visible, and so are the runs that hold tiles 128 - 128 // 2 to 191. `window_id`: window numbers start at 0 in every slide and rise by 0 or 1 from tile to tile; a window holds 1 to 128 consecutive tiles; the last tile of every slide is in window 2 * 64 - 2.
All inputs are finite; a program needn't handle non-finite values.
Results may differ from the reference program's by a relative error of at most 0.019.
Values may be sent and summed in bfloat16 or wider, within the bound.
No kernel may reach another device: no remote copies, remote signals or barrier semaphores. Data moves between devices by JAX's collectives and lax.ppermute only.
A program may use at most 64 MiB of HBM per device.

```python
import math
import jax
import jax.numpy as jnp
from jax import lax

D = 512
HEADS = 8
TILE_DEV = 128
WIN = 128
SLIDES = 8
TILES = 8192
VIS = 2048
N_GRID = 64


def draw_visible(key, part):
    key = jax.random.fold_in(key, 11)
    run_len = TILE_DEV // 4
    runs_all = TILES // run_len
    chosen_count = VIS // run_len
    half = WIN // 2

    def one_slide(slide_key):
        first, second = jax.random.split(slide_key)
        full_shard = jax.random.randint(first, (), 0, TILES // TILE_DEV)
        logit_scores = jax.random.permutation(second, runs_all)
        run_ids = jnp.arange(runs_all)
        edge_run = (run_ids * run_len < TILE_DEV + half) & ((run_ids + 1) * run_len > TILE_DEV - half)
        forced = (run_ids // 4 == full_shard) | edge_run
        logit_scores = jnp.where(forced, runs_all + run_ids, logit_scores)
        picked = jnp.sort(lax.top_k(logit_scores, chosen_count)[1])
        tile_list = (picked[:, None] * run_len + jnp.arange(run_len)[None, :]).reshape(-1)
        return tile_list.astype(jnp.int32)
    return jax.vmap(one_slide)(jax.random.split(key, SLIDES))


def draw_window_id(key, part):
    key = jax.random.fold_in(key, 13)
    half = WIN // 2
    frame_count = TILES // WIN
    spots = jnp.arange(TILES, dtype=jnp.int32)
    shifted = spots - half
    frame_of = jnp.where(spots >= half, shifted // WIN, 0)
    offset_in = jnp.where(spots >= half, shifted % WIN, 0)
    frame_start = (spots == 0) | (spots >= half) & (offset_in == 0)
    full_frame = (spots >= half) & (half + (frame_of + 1) * WIN <= TILES)
    protected_frame = frame_of == (TILE_DEV - half - half) // WIN
    split_at = jax.random.randint(key, (SLIDES, frame_count), 1, WIN)
    chosen = jnp.take(split_at, jnp.clip(frame_of, 0, frame_count - 1), axis=1)
    extra = (offset_in[None, :] == chosen) & (full_frame & jnp.logical_not(protected_frame))[None, :]
    starts = frame_start[None, :] | extra
    return (jnp.cumsum(starts.astype(jnp.int32), axis=1) - 1).astype(jnp.int32)


def drawn_weights(key):
    return jnp.clip(jax.random.normal(key, (D, 3 * D), jnp.float32), -4.0, 4.0) * D ** (-0.5)


def draw_enc_qkv(key, part):
    key = jax.random.fold_in(key, 5)
    return drawn_weights(key).astype(jnp.bfloat16)


def draw_dec_qkv(key, part):
    key = jax.random.fold_in(key, 7)
    return drawn_weights(key).astype(jnp.bfloat16)


def block_levels(rng, dims, shards, smallest, high):
    loudness, own = 1.0, jax.random.fold_in(rng, 6)
    for dim, parts in shards:
        heights = jnp.exp(jax.random.uniform(jax.random.fold_in(own, dim), (parts,), jnp.float32, smallest / len(shards), high / len(shards)))
        loudness = loudness * jnp.repeat(heights, dims[dim] // parts).reshape([-1 if axis == dim else 1 for axis in range(len(dims))])
    return loudness


def scatter_about(rng, dims, spread, reach, cuts=(), held_as=jnp.bfloat16):
    gain = block_levels(rng, dims, cuts, -0.22, 0.18) if cuts else 1.0
    array = jax.random.normal(rng, dims, jnp.float32) * spread * gain
    return jnp.minimum(jnp.maximum(array, -reach), reach).astype(held_as)


def setup_inputs(seed: int = 0) -> dict:
    keys = jax.random.split(jax.random.key(seed), 10)
    return {
        "embeddings": scatter_about(keys[0], (SLIDES, TILES, D), 1.0, 6.0, ((0, 8), (1, 64))),
        "visible": draw_visible(jax.random.fold_in(keys[9], 71), 0),
        "window_id": draw_window_id(jax.random.fold_in(keys[9], 71), 0),
        "output_gradient": scatter_about(keys[3], (SLIDES, TILES, D), 1.0, 6.0, ((0, 8), (1, 64))),
        "mask_token": scatter_about(keys[4], (D,), 1.0, 4.0, (), jnp.float32),
        "enc_qkv": draw_enc_qkv(jax.random.fold_in(keys[9], 71), 0),
        "enc_out": scatter_about(keys[6], (D, D), D ** -0.5, 0.25),
        "dec_qkv": draw_dec_qkv(jax.random.fold_in(keys[9], 71), 0),
        "decoder_projected": scatter_about(keys[8], (D, D), D ** -0.5, 0.25),
    }


EPS = 1e-06

def rms_f(values):
    return values * lax.rsqrt(lax.optimization_barrier(jnp.mean(values * values, axis=-1, keepdims=True)) + EPS)

def attend(queries, key_vecs, values, allowed, head_count):
    shape_q = queries.shape
    head_width = shape_q[-1] // head_count
    query_per_head = queries.reshape(shape_q[:-1] + (head_count, head_width))
    key_per_head = key_vecs.reshape(key_vecs.shape[:-1] + (head_count, head_width))
    value_per_head = values.reshape(values.shape[:-1] + (head_count, head_width))
    logit_scores = jnp.einsum('...vys,...rys->...yvr', query_per_head, key_per_head) * (1.0 / math.sqrt(head_width))
    if allowed is not None:
        logit_scores = jnp.where(allowed[..., None, :, :], logit_scores, -1e+30)
    row_top = lax.stop_gradient(lax.optimization_barrier(jnp.max(logit_scores, axis=-1, keepdims=True)))
    weights = jnp.exp(logit_scores - row_top)
    attention_probs = (weights / lax.optimization_barrier(jnp.sum(weights, axis=-1, keepdims=True))).astype(jnp.bfloat16)
    attention_probs = lax.optimization_barrier(attention_probs).astype(jnp.float32)
    attended_rows = jnp.einsum('...wvy,...ywj->...vwj', attention_probs, value_per_head)
    return attended_rows.reshape(shape_q).astype(jnp.bfloat16)

def encoder_block(tokens, enc_qkv, enc_out):
    width = tokens.shape[-1]
    residual = tokens.astype(jnp.float32)
    normed = rms_f(residual).astype(jnp.bfloat16)
    projected = jnp.dot(normed, enc_qkv, preferred_element_type=jnp.float32).astype(jnp.bfloat16)
    projected = lax.optimization_barrier(projected).astype(jnp.float32)
    attended_rows = attend(projected[..., :width], projected[..., width:2 * width], projected[..., 2 * width:], None, HEADS)
    hidden = residual + jnp.dot(attended_rows, enc_out, preferred_element_type=jnp.float32)
    return (hidden.astype(jnp.bfloat16), attended_rows)

def decoder_grads(inputs, window, cotangent, dec_qkv, decoder_projected):
    length, width = inputs.shape
    block = math.gcd(length, 256)
    normed = rms_f(inputs).astype(jnp.bfloat16)
    queries = jnp.dot(normed, dec_qkv[:, :width], preferred_element_type=jnp.float32).astype(jnp.bfloat16)
    keyvals = jnp.dot(normed, dec_qkv[:, width:], preferred_element_type=jnp.float32).astype(jnp.bfloat16)
    queries, keyvals = lax.optimization_barrier((queries, keyvals))
    padded = jnp.pad(keyvals, ((WIN, WIN), (0, 0)))
    padded_ids = jnp.pad(window, (WIN, WIN), constant_values=-1)
    dcontext = jnp.dot(cotangent, decoder_projected.T, preferred_element_type=jnp.float32).astype(jnp.bfloat16)

    def step(carry, index):
        start = (index * block).astype(jnp.int32)
        query_block = lax.dynamic_slice_in_dim(queries, start, block, 0).astype(jnp.float32)
        keyval_block = lax.dynamic_slice_in_dim(padded, start, block + 2 * WIN, 0).astype(jnp.float32)
        query_ids = lax.dynamic_slice_in_dim(window, start, block, 0)
        key_ids = lax.dynamic_slice_in_dim(padded_ids, start, block + 2 * WIN, 0)
        allowed = query_ids[:, None] == key_ids[None, :]

        def window_attend(query_f, keyval_f):
            return attend(query_f, keyval_f[:, :width], keyval_f[:, width:], allowed, HEADS)
        attended_rows, back = jax.vjp(window_attend, query_block, keyval_block)
        grad_q, grad_kv = back(lax.dynamic_slice_in_dim(dcontext, start, block, 0))
        current = lax.dynamic_slice_in_dim(carry, start, block + 2 * WIN, 0)
        carry = lax.dynamic_update_slice_in_dim(carry, current + grad_kv, start, 0)
        return (carry, (grad_q, attended_rows))
    total_kv, (grad_q, attended_rows) = lax.scan(step, jnp.zeros((length + 2 * WIN, 2 * width), jnp.float32), jnp.arange(length // block, dtype=jnp.int32))
    grad_q = grad_q.reshape(length, width)
    attended_rows = attended_rows.reshape(length, width)
    grad_kv = total_kv[WIN:WIN + length]
    dnormed = jnp.dot(grad_q, dec_qkv[:, :width].T, precision=lax.Precision.HIGHEST, preferred_element_type=jnp.float32)
    dnormed = dnormed + jnp.dot(grad_kv, dec_qkv[:, width:].T, precision=lax.Precision.HIGHEST, preferred_element_type=jnp.float32)
    _, norm_back = jax.vjp(rms_f, inputs)
    dinputs = norm_back(dnormed)[0] + cotangent.astype(jnp.float32)
    grad_weight = jnp.dot(attended_rows.T, cotangent, preferred_element_type=jnp.float32)
    return (dinputs, grad_weight)

def reference(embeddings, visible, window_id, output_gradient, mask_token, enc_qkv, enc_out, dec_qkv, decoder_projected):

    def one_slide(operands):
        tile_rows, vis_list, window, cotangent = operands
        tokens = tile_rows[vis_list]
        grouped = tokens.reshape(VIS // N_GRID, N_GRID, D).transpose(1, 0, 2)

        def encode(inputs):
            return encoder_block(inputs, enc_qkv, enc_out)
        encoded, enc_back, encoder_attended = jax.vjp(encode, grouped, has_aux=True)
        encoded = lax.optimization_barrier(encoded)
        flat = encoded.transpose(1, 0, 2).reshape(VIS, D)
        inputs = jnp.broadcast_to(mask_token, (TILES, D)).astype(jnp.float32)
        inputs = inputs.at[vis_list].set(flat.astype(jnp.float32))
        dinputs, grad_dec = decoder_grads(inputs, window, cotangent, dec_qkv, decoder_projected)
        grad_flat = dinputs[vis_list].astype(jnp.bfloat16)
        grad_grouped = grad_flat.reshape(VIS // N_GRID, N_GRID, D).transpose(1, 0, 2)
        grad_enc = jnp.dot(encoder_attended.reshape(-1, D).T, grad_grouped.reshape(-1, D), preferred_element_type=jnp.float32)
        grad_tokens, = enc_back(grad_grouped)
        token_flat = grad_tokens.transpose(1, 0, 2).reshape(VIS, D)
        grad_tiles = jnp.zeros((TILES, D), jnp.bfloat16).at[vis_list].set(token_flat)
        return (grad_tiles, grad_enc, grad_dec)
    grad_tiles, enc_parts, dec_parts = lax.map(one_slide, (embeddings, visible, window_id, output_gradient))
    return (grad_tiles, lax.optimization_barrier(jnp.sum(enc_parts, axis=0)), lax.optimization_barrier(jnp.sum(dec_parts, axis=0)))
```

```python
import functools

import jax
import jax.numpy as jnp
from jax import lax
from jax.experimental import pallas as pl
from jax.experimental.pallas import tpu as pltpu
from jax.sharding import PartitionSpec as P

HEADS = 8
HEAD = 64
D = 512
TILE = 128
FRAME = 256
RUN = 32
GROUPS = 64
TOKENS = 32
EPS = 1e-06
SCALE = 0.125
NEG = -1e30
BF = jnp.bfloat16
F32 = jnp.float32
I32 = jnp.int32


def nn(a, b):
    return lax.dot_general(a, b, (((1,), (0,)), ((), ())), preferred_element_type=F32)


def nt(a, b):
    return lax.dot_general(a, b, (((1,), (1,)), ((), ())), preferred_element_type=F32)


def tn(a, b):
    return lax.dot_general(a, b, (((0,), (0,)), ((), ())), preferred_element_type=F32)


def iota(shape, dim):
    return lax.broadcasted_iota(I32, shape, dim)


def onehot(cond):
    return jnp.where(cond, 1.0, 0.0).astype(BF)


def own_slots(counts, spots):
    base = counts[0]
    place = spots // RUN
    slot = jnp.full(spots.shape, -1, I32)
    for p in range(TILE // RUN):
        rank = counts[p] + spots % RUN
        target = (rank % GROUPS) * 2 + (rank - base) // GROUPS
        slot = jnp.where((place == p) & (counts[p + 1] > counts[p]), target, slot)
    return slot


def send_tokens_kernel(visible_ref, emb_ref, out_ref):
    first = lax.axis_index("grid") * TILE
    visible = visible_ref[...]
    counts = []
    for p in range(TILE // RUN + 1):
        below = jnp.where(visible < first + p * RUN, 1.0, 0.0)
        counts.append(jnp.sum(jnp.sum(below, axis=0, keepdims=True), axis=1, keepdims=True).astype(I32))
    slot = own_slots(counts, iota((1, TILE), 1))
    rows = iota((GROUPS * 8, TILE), 0)
    total = jnp.zeros((GROUPS * 8, TILE), F32)
    for part in range(4):
        total += nn(onehot(rows == slot * 4 + part), emb_ref[:, part * 128 : (part + 1) * 128])
    out_ref[...] = total.astype(BF)


def per_head(rows):
    stacked = jnp.concatenate([rows] * HEADS, axis=0)
    shape = stacked.shape
    same = iota(shape, 0) // TOKENS == iota(shape, 1) // HEAD
    return jnp.where(same, stacked.astype(F32), 0.0).astype(BF)


def fold_heads(stacked):
    shape = stacked.shape
    same = iota(shape, 0) // TOKENS == iota(shape, 1) // HEAD
    kept = jnp.where(same, stacked, 0.0)
    total = kept[:TOKENS]
    for h in range(1, HEADS):
        total += kept[h * TOKENS : (h + 1) * TOKENS]
    return total


def group_match(low_ref, high_ref):
    ranks = iota((TOKENS, GROUPS * 8), 0) * GROUPS + lax.axis_index("grid")
    return (ranks >= low_ref[...]) & (ranks < high_ref[...])


def encode_kernel(recv_ref, low1_ref, high1_ref, low2_ref, high2_ref, qkv_ref, out_ref, tokens_ref, proj_ref, probs_ref):
    match1 = group_match(low1_ref, high1_ref)
    lanes = iota((TOKENS, GROUPS * 8), 1)
    recv = recv_ref[...]
    tokens = jnp.concatenate(
        [nn(onehot(match1 & (lanes % 4 == part)), recv) for part in range(4)], axis=1
    )
    tokens_ref[...] = tokens
    normed = (tokens * lax.rsqrt(jnp.mean(tokens * tokens, axis=1, keepdims=True) + EPS)).astype(BF)
    proj = nn(normed, qkv_ref[...]).astype(BF)
    proj_ref[...] = proj
    scores = nt(per_head(proj[:, :D]), proj[:, D : 2 * D]) * SCALE
    weights = jnp.exp(scores - jnp.max(scores, axis=1, keepdims=True))
    probs = weights / jnp.sum(weights, axis=1, keepdims=True)
    probs_ref[...] = probs
    context = fold_heads(nn(probs.astype(BF), proj[:, 2 * D :])).astype(BF)
    match2 = group_match(low2_ref, high2_ref)
    out = tn(onehot(match2 & (lanes % 2 == 0)), context[:, :256])
    out += tn(onehot(match2 & (lanes % 2 == 1)), context[:, 256:])
    out_ref[...] = out.astype(BF)


def decode_kernel(
    info_ref,
    recv_ref,
    embt_ref,
    og_ref,
    ogt_ref,
    wid_row_ref,
    wid_col_ref,
    mask_ref,
    enc_out_t_ref,
    qkv_t_ref,
    qkv_ref,
    proj_ref,
    out_ref,
    part_ref,
    dqkv_ref,
    ctx_ref,
):
    first = lax.axis_index("grid") * TILE
    begin, end = info_ref[9], info_ref[10]
    low, high = info_ref[11] - first, info_ref[12] - first
    lane = iota((1, FRAME), 1)
    place = lane // RUN
    rank = jnp.full((1, FRAME), -1, I32)
    for p in range(FRAME // RUN):
        seen = (place == p) & (info_ref[p + 1] > info_ref[p])
        rank = jnp.where(seen, info_ref[p] + lane % RUN, rank)
    live = (rank >= begin) & (rank < end)
    slot = jnp.where(live, (rank % GROUPS) * 4 + (rank - begin) // GROUPS, -1)
    owned = (lane >= low) & (lane < high)
    rows = iota((GROUPS * 8, FRAME), 0)
    pick = [onehot(rows == slot * 2 + half) for half in range(2)]

    recv = recv_ref[...]
    ctx_enc = jnp.concatenate([tn(recv, pick[half]) for half in range(2)], axis=0).astype(BF)
    encoded = (embt_ref[...].astype(F32) + nn(enc_out_t_ref[...], ctx_enc)).astype(BF)
    x = jnp.where(live, encoded.astype(F32), mask_ref[...])
    inv = lax.rsqrt(jnp.mean(x * x, axis=0, keepdims=True) + EPS)
    normed = (x * inv).astype(BF)
    qkv = nn(qkv_t_ref[...], normed).astype(BF)
    og_t = jnp.where(owned, ogt_ref[...].astype(F32), 0.0)
    dctx = nn(proj_ref[...], og_t.astype(BF)).astype(BF)
    keys = qkv[D : 2 * D].T
    vals = qkv[2 * D :].T

    col = iota((FRAME, 1), 0)
    owned_col = (col >= low) & (col < high)
    same = jnp.where(owned_col, wid_col_ref[...], -1 - col) == jnp.where(owned, wid_row_ref[...], -1 - lane)
    for h in range(HEADS):
        spot = slice(h * HEAD, (h + 1) * HEAD)
        q_t, k_t, v_t = qkv[spot], qkv[D + h * HEAD : D + (h + 1) * HEAD], qkv[2 * D + h * HEAD : 2 * D + (h + 1) * HEAD]
        d_t = dctx[spot]
        scores = jnp.where(same, nn(keys[:, spot], q_t) * SCALE, NEG)
        weights = jnp.exp(scores - jnp.max(scores, axis=0, keepdims=True))
        probs = weights * (1.0 / jnp.sum(weights, axis=0, keepdims=True))
        probs_b = probs.astype(BF)
        ctx_ref[spot, :] = jnp.where(owned, nn(v_t, probs_b), 0.0).astype(BF)
        dprobs = nn(vals[:, spot], d_t).astype(BF).astype(F32)
        inner = jnp.sum(probs * dprobs, axis=0, keepdims=True)
        dscores = (probs * (dprobs - inner) * SCALE).astype(BF)
        dqkv_ref[spot, :] = nn(k_t, dscores).astype(BF)
        dqkv_ref[D + h * HEAD : D + (h + 1) * HEAD, :] = nt(q_t, dscores).astype(BF)
        dqkv_ref[2 * D + h * HEAD : 2 * D + (h + 1) * HEAD, :] = nt(d_t, probs_b).astype(BF)

    dnormed = nn(qkv_ref[...], dqkv_ref[...])
    slope = inv * inv * inv * jnp.mean(x * dnormed, axis=0, keepdims=True)
    dx = (inv * dnormed - x * slope + og_t).astype(BF)
    dx_rows = dx.T
    out = nn(pick[0], dx_rows[:, :256]) + nn(pick[1], dx_rows[:, 256:])
    out_ref[...] = out.astype(BF)
    grad_enc = nn(ctx_enc, dx_rows).astype(BF)
    grad_dec = nn(ctx_ref[...], og_ref[...]).astype(BF)
    for s in range(8):
        spot = slice(s * 64, (s + 1) * 64)
        part_ref[s] = jnp.concatenate([grad_enc[:, spot], grad_dec[:, spot]], axis=1)


def encode_back_kernel(
    recv_ref, parts_ref, low1_ref, high1_ref, low2_ref, high2_ref, tokens_ref, proj_ref, probs_ref, qkv_ref, enc_out_ref, out_ref
):
    match2 = group_match(low2_ref, high2_ref)
    lanes = iota((TOKENS, GROUPS * 8), 1)
    recv = recv_ref[...]
    grad = jnp.concatenate(
        [nn(onehot(match2 & (lanes % 2 == half)), recv) for half in range(2)], axis=1
    )
    proj = proj_ref[...]
    probs = probs_ref[...]
    dctx = per_head(nt(grad.astype(BF), enc_out_ref[...]).astype(BF))
    dprobs = nt(dctx, proj[:, 2 * D :]).astype(BF).astype(F32)
    inner = jnp.sum(probs * dprobs, axis=1, keepdims=True)
    dscores = (probs * (dprobs - inner) * SCALE).astype(BF)
    dq = fold_heads(nn(dscores, proj[:, D : 2 * D]))
    dk = tn(dscores, per_head(proj[:, :D]))
    dv = tn(probs.astype(BF), dctx)
    dproj = jnp.concatenate([dq, dk, dv], axis=1).astype(BF)
    dnormed = nt(dproj, qkv_ref[...]).astype(BF).astype(F32)
    x = tokens_ref[...]
    inv = lax.rsqrt(jnp.mean(x * x, axis=1, keepdims=True) + EPS)
    slope = inv * inv * inv * jnp.mean(x * dnormed, axis=1, keepdims=True)
    dtokens = (grad + (inv * dnormed - x * slope)).astype(BF)
    match1 = group_match(low1_ref, high1_ref)
    out = jnp.zeros((GROUPS * 8, 128), F32)
    for part in range(4):
        out += tn(onehot(match1 & (lanes % 4 == part)), dtokens[:, part * 128 : (part + 1) * 128])
    out_ref[:, :128] = out.astype(BF)
    total = parts_ref[0].astype(F32)
    for s in range(1, 8):
        total += parts_ref[s].astype(F32)
    out_ref[:, 128:] = total.astype(BF)


def finish_kernel(info_ref, recv_ref, tiles_ref, enc_ref, dec_ref):
    counts = [info_ref[p] for p in range(TILE // RUN + 1)]
    slot = own_slots(counts, iota((TILE, 1), 0))
    lanes = iota((TILE, GROUPS * 8), 1)
    recv = recv_ref[:, :128]
    for part in range(4):
        tiles_ref[:, part * 128 : (part + 1) * 128] = nn(onehot(lanes == slot * 4 + part), recv).astype(BF)
    rows = recv_ref[:, 128:].astype(F32).reshape(GROUPS, 8, 128)
    total = jnp.sum(rows, axis=0)
    enc_ref[...] = total[:, :64]
    dec_ref[...] = total[:, 64:]


VM = pl.BlockSpec(memory_space=pltpu.VMEM)
SM = pl.BlockSpec(memory_space=pltpu.SMEM)


def call(kernel, shapes, args, name, scratch=(), scalars=0):
    outs = [jax.ShapeDtypeStruct(s, t) for s, t in shapes]
    return pl.pallas_call(
        kernel,
        out_shape=outs,
        in_specs=[SM] * scalars + [VM] * (len(args) - scalars),
        out_specs=[VM] * len(outs),
        scratch_shapes=list(scratch),
        compiler_params=pltpu.CompilerParams(vmem_limit_bytes=40 * 1024 * 1024),
        name=name,
    )(*args)


def exchange(rows, axis):
    return lax.all_to_all(rows, axis, split_axis=0, concat_axis=0, tiled=True)


def slot_bounds(starts, turns):
    low = starts[:-1, None] + GROUPS * jnp.arange(turns, dtype=I32)[None, :]
    high = jnp.minimum(low + GROUPS, starts[1:, None])
    wide = [jnp.repeat(b.reshape(-1), 8 // turns).reshape(1, GROUPS * 8) for b in (low, high)]
    return wide


def shards(
    embeddings,
    visible,
    window_id,
    output_gradient,
    mask_token,
    enc_qkv,
    enc_out,
    dec_qkv,
    decoder_projected,
):
    emb = embeddings[0]
    og = output_gradient[0]
    (send1,) = call(
        send_tokens_kernel,
        [((GROUPS * 8, 128), BF)],
        (visible.reshape(16, 128), emb),
        "send_tokens",
    )
    recv1 = exchange(send1, "grid")

    d = lax.axis_index("grid")
    runs = visible.reshape(GROUPS, RUN)[:, 0] // RUN
    edge = jnp.arange(GROUPS + 1, dtype=I32)
    start1 = RUN * jnp.sum((runs[None, :] < 4 * edge[:, None]).astype(I32), axis=1)
    wid = window_id.reshape(GROUPS, TILE)
    before = jnp.concatenate([jnp.full((1,), -1, I32), wid[:-1, -1]])
    head = edge[:-1] * TILE + jnp.sum((wid == before[:, None]).astype(I32), axis=1)
    head = jnp.concatenate([head, jnp.full((1,), GROUPS * TILE, I32)])
    start2 = jnp.sum(jnp.clip(head[:, None] - RUN * runs[None, :], 0, RUN), axis=1)
    low1, high1 = slot_bounds(start1, 2)
    low2, high2 = slot_bounds(start2, 4)
    frame_runs = 4 * d + jnp.arange(9, dtype=I32)
    frame_counts = RUN * jnp.sum((runs[None, :] < frame_runs[:, None]).astype(I32), axis=1)
    info = jnp.concatenate(
        [
            frame_counts,
            lax.dynamic_slice_in_dim(start2, d, 2),
            lax.dynamic_slice_in_dim(head, d, 2),
        ]
    )
    wid_pad = jnp.concatenate([window_id[0], jnp.full((TILE,), -1, I32)])
    wid_frame = lax.dynamic_slice_in_dim(wid_pad, d * TILE, FRAME)

    halo = lax.ppermute(
        jnp.concatenate([emb, og], axis=1), "grid", [(i + 1, i) for i in range(GROUPS - 1)]
    )
    emb_t = jnp.concatenate([emb, halo[:, :D]], axis=0).T
    og_frame = jnp.concatenate([og, halo[:, D:]], axis=0)

    send2, tokens, proj, probs = call(
        encode_kernel,
        [((GROUPS * 8, 256), BF), ((TOKENS, D), F32), ((TOKENS, 3 * D), BF), ((HEADS * TOKENS, TOKENS), F32)],
        (recv1, low1, high1, low2, high2, enc_qkv),
        "encode",
    )
    recv2 = exchange(send2, "grid")
    send3, parts = call(
        decode_kernel,
        [((GROUPS * 8, 256), BF), ((8, D, 128), BF)],
        (
            info,
            recv2,
            emb_t,
            og_frame,
            og_frame.T,
            wid_frame[None, :],
            wid_frame[:, None],
            mask_token[:, None],
            enc_out.T,
            dec_qkv.T,
            dec_qkv,
            decoder_projected,
        ),
        "decode",
        scratch=[pltpu.VMEM((3 * D, FRAME), BF), pltpu.VMEM((D, FRAME), BF)],
        scalars=1,
    )
    recv3 = exchange(send3, "grid")
    parts = exchange(parts, "slide")
    (send4,) = call(
        encode_back_kernel,
        [((GROUPS * 8, 256), BF)],
        (recv3, parts, low1, high1, low2, high2, tokens, proj, probs, enc_qkv, enc_out),
        "encode_back",
    )
    recv4 = exchange(send4, "grid")
    tiles, grad_enc, grad_dec = call(
        finish_kernel,
        [((TILE, D), BF), ((8, 64), F32), ((8, 64), F32)],
        (info, recv4),
        "finish",
        scalars=1,
    )
    return tiles[None], grad_enc, grad_dec


def solution(mesh):
    placed = (
        P("slide", "grid", None),
        P("slide", None),
        P("slide", None),
        P("slide", "grid", None),
        P(),
        P(),
        P(),
        P(),
        P(),
    )
    return jax.shard_map(
        shards,
        mesh=mesh,
        in_specs=placed,
        out_specs=(P("slide", "grid", None), P("grid", "slide"), P("grid", "slide")),
        check_vma=False,
    )
```

```python
import jax
import jax.numpy as jnp
from jax import lax
from jax.experimental import pallas as pl
from jax.experimental.pallas import tpu as pltpu
from jax.sharding import PartitionSpec as P

HEADS = 8
HEAD = 64
D = 512
TILE = 128
FRAME = 256
RUN = 32
GROUPS = 64
TOKENS = 32
EPS = 1e-06
SCALE = 0.125
NEG = -1e30
BF = jnp.bfloat16
F32 = jnp.float32
I32 = jnp.int32


def nn(a, b):
    return lax.dot_general(a, b, (((1,), (0,)), ((), ())), preferred_element_type=F32)


def nt(a, b):
    return lax.dot_general(a, b, (((1,), (1,)), ((), ())), preferred_element_type=F32)


def tn(a, b):
    return lax.dot_general(a, b, (((0,), (0,)), ((), ())), preferred_element_type=F32)


def iota(shape, dim):
    return lax.broadcasted_iota(I32, shape, dim)


def onehot(cond):
    return jnp.where(cond, 1.0, 0.0).astype(BF)


class Load:
    def __init__(self, source, held, sems, first, parts=1):
        self.held = held
        rows = held.shape[0] // parts
        spots = [slice(i * rows, (i + 1) * rows) for i in range(parts)]
        self.copies = [
            pltpu.make_async_copy(source.at[spot], held.at[spot], sems.at[first + i]) for i, spot in enumerate(spots)
        ]
        for copy in self.copies:
            copy.start()

    def __call__(self):
        for copy in self.copies:
            copy.wait()
        self.copies = []
        return self.held


def run_counts(visible_ref, limit):
    total = jnp.zeros(limit.shape, I32)
    for q in range(4):
        firsts = visible_ref[:, q * RUN : q * RUN + 1]
        total += jnp.sum(jnp.where(firsts < limit, 1, 0), axis=0, keepdims=True)
    return total


def frame_ranks(visible_ref, first, width):
    lane = iota((1, width), 1)
    limit = first + lane - (lane & (RUN - 1))
    seen = run_counts(visible_ref, limit)
    present = run_counts(visible_ref, limit + RUN) > seen
    return seen * RUN + (lane & (RUN - 1)), present


def own_slots(visible_ref, first):
    rank, present = frame_ranks(visible_ref, first, TILE)
    base = RUN * run_counts(visible_ref, jnp.broadcast_to(first, (1, TILE)))
    return jnp.where(present, (rank & (GROUPS - 1)) * 2 + ((rank - base) >> 6), -1)


def send_tokens_kernel(visible_hbm, emb_hbm, out_ref, visible_b, emb_b, sems):
    visible = Load(visible_hbm, visible_b, sems, 0)
    emb = Load(emb_hbm, emb_b, sems, 1)
    slot = own_slots(visible(), lax.axis_index("grid") * TILE)
    rows = iota((GROUPS * 8, TILE), 0)
    picks = [onehot(rows == slot * 4 + part) for part in range(4)]
    emb_ref = emb()
    total = jnp.zeros((GROUPS * 8, TILE), F32)
    for part in range(4):
        total += nn(picks[part], emb_ref[:, part * 128 : (part + 1) * 128])
    out_ref[...] = total.astype(BF)


def plan_kernel(visible_ref, wid_ref, enc_qkv_ref, marks_ref, enc_ref):
    enc_ref[...] = enc_qkv_ref[...]
    d = lax.axis_index("grid")
    first = d * TILE
    lane = iota((1, GROUPS * 8), 1)
    peer = lane >> 3
    start1 = RUN * run_counts(visible_ref, peer * TILE)
    stop1 = RUN * run_counts(visible_ref, peer * TILE + TILE)
    low1 = start1 + GROUPS * ((lane >> 2) & 1)
    marks_ref[0:1, :] = low1
    marks_ref[1:2, :] = jnp.minimum(low1 + GROUPS, stop1)

    wid = wid_ref[...]
    last = wid[:, TILE - 1 :]
    before = jnp.concatenate([jnp.full((1, 1), -1, I32), last[:-1]], axis=0)
    more = jnp.sum(jnp.where(wid == before, 1.0, 0.0), axis=1, keepdims=True).astype(I32)
    head = iota((GROUPS, 1), 0) * TILE + more
    rows = iota((GROUPS, GROUPS * 8), 0)
    begin = jnp.sum(jnp.where(rows == peer, head, 0), axis=0, keepdims=True)
    end = jnp.sum(jnp.where(rows == peer + 1, head, 0), axis=0, keepdims=True)
    end = jnp.where(peer == GROUPS - 1, GROUPS * TILE, end)

    def visible_below(tile):
        total = jnp.zeros(tile.shape, I32)
        for q in range(4):
            firsts = visible_ref[:, q * RUN : q * RUN + 1]
            total += jnp.sum(jnp.clip(tile - firsts, 0, RUN), axis=0, keepdims=True)
        return total

    start2, stop2 = visible_below(begin), visible_below(end)
    low2 = start2 + GROUPS * ((lane >> 1) & 3)
    marks_ref[2:3, :] = low2
    marks_ref[3:4, :] = jnp.minimum(low2 + GROUPS, stop2)
    marks_ref[4:8, :] = jnp.zeros((4, GROUPS * 8), I32)

    def mine(values):
        return jnp.sum(jnp.where(lane == d * 8, values.astype(F32), 0.0), axis=1, keepdims=True).astype(I32)

    start2, stop2, begin, end = mine(start2), mine(stop2), mine(begin), mine(end)
    rank, present = frame_ranks(visible_ref, first, FRAME)
    spot = iota((1, FRAME), 1)
    live = present & (rank >= start2) & (rank < stop2)
    owned = (first + spot >= begin) & (first + spot < end)
    marks_ref[4:5, :FRAME] = jnp.where(live, (rank & (GROUPS - 1)) * 4 + ((rank - start2) >> 6), -1)
    marks_ref[5:6, :FRAME] = jnp.where(owned, 1, 0)
    own = wid_ref[pl.ds(d, 1), :]
    after = wid_ref[pl.ds(jnp.minimum(d + 1, GROUPS - 1), 1), :]
    marks_ref[6:7, :FRAME] = jnp.where(owned, jnp.concatenate([own, after], axis=1), -1 - spot)
    marks_ref[7:8, :TILE] = own_slots(visible_ref, first)


OUT_T, BOTH, MORE, QKV, OG_ROWS, PACKED = 1536, 0, 512, 1024, 2560, 18432


def prepare_kernel(marks_ref, emb_ref, og_ref, halo_ref, proj_ref, enc_out_ref, qkv_ref, flipped_ref, packed_ref, held, sems):
    def ship(first, last, sem):
        copy = pltpu.make_async_copy(held.at[first:last], packed_ref.at[first:last], sems.at[sem])
        copy.start()
        return copy

    for i in range(3):
        held[QKV + i * D : QKV + (i + 1) * D, :] = qkv_ref[:, i * D : (i + 1) * D]
    copies = [ship(QKV, OG_ROWS, 0)]
    flipped_ref[:OUT_T, :] = qkv_ref[...].T
    flipped_ref[OUT_T:, :] = enc_out_ref[...].T
    owned = marks_ref[5:6, :FRAME] > 0
    held[OG_ROWS : OG_ROWS + TILE, :] = og_ref[...]
    held[OG_ROWS + TILE : OG_ROWS + FRAME, :] = halo_ref[:, D:]
    og_t = jnp.concatenate([og_ref[...].T, halo_ref[:, D:].T], axis=1).astype(F32)
    og_t = jnp.where(owned, og_t, 0.0).astype(BF)
    held[BOTH:MORE, :FRAME] = nn(proj_ref[...], og_t).astype(BF)
    held[BOTH:MORE, FRAME:] = og_t
    held[MORE : MORE + D, :FRAME] = jnp.concatenate([emb_ref[...].T, halo_ref[:, :D].T], axis=1)
    across = jnp.broadcast_to(marks_ref[6:7, :FRAME], (FRAME, FRAME))
    held[MORE : MORE + FRAME, FRAME:] = jnp.where(across == across.T, 0.0, NEG).astype(BF)
    held[MORE + FRAME : MORE + D, FRAME:] = jnp.zeros((FRAME, FRAME), BF)
    copies.append(ship(OG_ROWS, OG_ROWS + FRAME, 1))
    copies.append(ship(BOTH, QKV, 2))
    for copy in copies:
        copy.wait()


def per_head(rows):
    stacked = jnp.concatenate([rows] * HEADS, axis=0)
    shape = stacked.shape
    same = iota(shape, 0) // TOKENS == iota(shape, 1) // HEAD
    return jnp.where(same, stacked.astype(F32), 0.0).astype(BF)


def fold_heads(stacked):
    shape = stacked.shape
    same = iota(shape, 0) // TOKENS == iota(shape, 1) // HEAD
    kept = jnp.where(same, stacked, 0.0)
    total = kept[:TOKENS]
    for h in range(1, HEADS):
        total += kept[h * TOKENS : (h + 1) * TOKENS]
    return total


def group_match(bounds_ref, row):
    ranks = iota((TOKENS, GROUPS * 8), 0) * GROUPS + lax.axis_index("grid")
    return (ranks >= bounds_ref[row : row + 1, :]) & (ranks < bounds_ref[row + 1 : row + 2, :])


def encoder_probs(queries, keys):
    scores = nt(per_head(queries), keys) * SCALE
    weights = jnp.exp(scores - jnp.max(scores, axis=1, keepdims=True))
    return weights / jnp.sum(weights, axis=1, keepdims=True)


def encode_kernel(recv_ref, marks_ref, weight_ref, out_ref, kept_ref):
    match1 = group_match(marks_ref, 0)
    lanes = iota((TOKENS, GROUPS * 8), 1)
    recv = recv_ref[...]
    x = jnp.concatenate([nn(onehot(match1 & (lanes % 4 == part)), recv) for part in range(4)], axis=1)
    kept_ref[:TOKENS, :] = x.astype(BF)
    normed = (x * lax.rsqrt(jnp.mean(x * x, axis=1, keepdims=True) + EPS)).astype(BF)
    qkv = nn(normed, weight_ref[...]).astype(BF)
    for i in range(3):
        kept_ref[(i + 1) * TOKENS : (i + 2) * TOKENS, :] = qkv[:, i * D : (i + 1) * D]
    soft = encoder_probs(qkv[:, :D], qkv[:, D : 2 * D])
    context = fold_heads(nn(soft.astype(BF), qkv[:, 2 * D :])).astype(BF)
    match2 = group_match(marks_ref, 2)
    out = tn(onehot(match2 & (lanes % 2 == 0)), context[:, :256])
    out += tn(onehot(match2 & (lanes % 2 == 1)), context[:, 256:])
    out_ref[...] = out.astype(BF)


def decode_kernel(marks_ref, recv_ref, mask_ref, flipped_ref, packed, out_ref, keep_ref, send_ref, more_b, both_b, qkv_b, og_b, dqkv_ref, ctx_ref, sems):
    more = Load(packed.at[MORE:QKV], more_b, sems, 0)
    both = Load(packed.at[BOTH:MORE], both_b, sems, 1)
    qkv_w = Load(packed.at[QKV:OG_ROWS], qkv_b, sems, 2)
    og_rows = Load(packed.at[OG_ROWS : OG_ROWS + FRAME], og_b, sems, 3)
    slot = marks_ref[4:5, :FRAME]
    live = slot >= 0
    owned = marks_ref[5:6, :FRAME] > 0
    blank = jnp.broadcast_to(mask_ref[...], (TILE, D)).T[:, :1]
    rows = iota((GROUPS * 8, FRAME), 0)
    pick = [onehot(rows == slot * 2 + half) for half in range(2)]
    recv = recv_ref[...]
    ctx_enc = jnp.concatenate([tn(recv, pick[half]) for half in range(2)], axis=0).astype(BF)
    delta = nn(flipped_ref[OUT_T:, :], ctx_enc)
    x = jnp.where(live, (more()[:, :FRAME].astype(F32) + delta).astype(BF).astype(F32), blank)
    inv = lax.rsqrt(jnp.mean(x * x, axis=0, keepdims=True) + EPS)
    normed = (x * inv).astype(BF)
    qkv = nn(flipped_ref[:OUT_T, :], normed).astype(BF)
    keys = qkv[D : 2 * D].T
    vals = qkv[2 * D :].T
    bias_rows = more()[:FRAME, FRAME:].astype(F32)
    both_b = both()
    for h in range(HEADS):
        spot = slice(h * HEAD, (h + 1) * HEAD)
        q_t, k_t, v_t = qkv[spot], qkv[D + h * HEAD : D + (h + 1) * HEAD], qkv[2 * D + h * HEAD : 2 * D + (h + 1) * HEAD]
        d_t = both_b[spot, :FRAME]
        scores = nn(keys[:, spot], q_t) * SCALE + bias_rows
        weights = jnp.exp(scores - jnp.max(scores, axis=0, keepdims=True))
        probs = weights * (1.0 / jnp.sum(weights, axis=0, keepdims=True))
        probs_b = probs.astype(BF)
        ctx_ref[spot, :] = jnp.where(owned, nn(v_t, probs_b), 0.0).astype(BF)
        dprobs = nn(vals[:, spot], d_t).astype(BF).astype(F32)
        inner = jnp.sum(probs * dprobs, axis=0, keepdims=True)
        dscores = (probs * (dprobs - inner) * SCALE).astype(BF)
        dqkv_ref[spot, :] = nn(k_t, dscores).astype(BF)
        dqkv_ref[D + h * HEAD : D + (h + 1) * HEAD, :] = nt(q_t, dscores).astype(BF)
        dqkv_ref[2 * D + h * HEAD : 2 * D + (h + 1) * HEAD, :] = nt(d_t, probs_b).astype(BF)

    weight_ref = qkv_w()
    dnormed = nn(weight_ref[:D, :], dqkv_ref[:D, :])
    for i in range(1, 3):
        dnormed += nn(weight_ref[i * D : (i + 1) * D, :], dqkv_ref[i * D : (i + 1) * D, :])
    slope = inv * inv * inv * jnp.mean(x * dnormed, axis=0, keepdims=True)
    dx = (inv * dnormed - x * slope + both_b[:, FRAME:].astype(F32)).astype(BF)
    dx_rows = dx.T
    out = nn(pick[0], dx_rows[:, :256]) + nn(pick[1], dx_rows[:, 256:])
    out_ref[...] = out.astype(BF)

    me = lax.axis_index("slide")
    even = (me & 1) == 0
    grad_enc = nn(ctx_enc, dx_rows).astype(BF)
    grad_dec = nn(ctx_ref[...], og_rows()[...]).astype(BF)

    def block(s):
        spot = slice(s * 64, (s + 1) * 64)
        return jnp.concatenate([grad_enc[:, spot], grad_dec[:, spot]], axis=1)

    for m in range(4):
        low, high = block(2 * m), block(2 * m + 1)
        j = m ^ (me >> 1)
        keep_ref[j] = jnp.where(even, low, high)
        send_ref[j] = jnp.where(even, high, low)


def add_kernel(keep_ref, recv_ref, *outs):
    for j in range(4):
        outs[j][...] = (keep_ref[j].astype(F32) + recv_ref[j].astype(F32)).astype(BF)


def encode_back_kernel(marks_ref, recv_ref, enc_out_ref, weight_ref, kept_ref, part0, part1, part2, part3, out_ref):
    queries, keys, values = [kept_ref[i * TOKENS : (i + 1) * TOKENS, :] for i in range(1, 4)]
    probs = encoder_probs(queries, keys)
    match2 = group_match(marks_ref, 2)
    lanes = iota((TOKENS, GROUPS * 8), 1)
    recv = recv_ref[...]
    grad = jnp.concatenate(
        [nn(onehot(match2 & (lanes % 2 == half)), recv) for half in range(2)], axis=1
    )
    dctx = per_head(nt(grad.astype(BF), enc_out_ref[...]).astype(BF))
    dprobs = nt(dctx, values).astype(BF).astype(F32)
    inner = jnp.sum(probs * dprobs, axis=1, keepdims=True)
    dscores = (probs * (dprobs - inner) * SCALE).astype(BF)
    dq = fold_heads(nn(dscores, keys))
    dk = tn(dscores, per_head(queries))
    dv = tn(probs.astype(BF), dctx)
    dproj = jnp.concatenate([dq, dk, dv], axis=1).astype(BF)
    dnormed = nt(dproj, weight_ref[...]).astype(BF).astype(F32)
    x = kept_ref[:TOKENS, :].astype(F32)
    inv = lax.rsqrt(jnp.mean(x * x, axis=1, keepdims=True) + EPS)
    slope = inv * inv * inv * jnp.mean(x * dnormed, axis=1, keepdims=True)
    dtokens = (grad + (inv * dnormed - x * slope)).astype(BF)
    match1 = group_match(marks_ref, 0)
    out = jnp.zeros((GROUPS * 8, 128), F32)
    for part in range(4):
        out += tn(onehot(match1 & (lanes % 4 == part)), dtokens[:, part * 128 : (part + 1) * 128])
    out_ref[:, :128] = out.astype(BF)
    parts = [p[...].astype(F32) for p in (part0, part1, part2, part3)]
    out_ref[:, 128:] = (parts[0] + parts[1] + parts[2] + parts[3]).astype(BF)


def finish_kernel(marks_ref, recv_ref, tiles_ref, enc_ref, dec_ref):
    slot = jnp.broadcast_to(marks_ref[7:8, :TILE], (TILE, TILE)).T[:, 0:1]
    lanes = iota((TILE, GROUPS * 8), 1)
    recv = recv_ref[:, :128]
    for part in range(4):
        tiles_ref[:, part * 128 : (part + 1) * 128] = nn(onehot(lanes == slot * 4 + part), recv).astype(BF)
    rows = recv_ref[:, 128:].astype(F32).reshape(GROUPS, 8, 128)
    total = jnp.sum(rows, axis=0)
    enc_ref[...] = total[:, :64]
    dec_ref[...] = total[:, 64:]


VM = pl.BlockSpec(memory_space=pltpu.VMEM)
HERE = pl.BlockSpec(memory_space=pl.ANY)


def call(kernel, outs, args, name, scratch=(), limit=16, flops=10**8, sems=0):
    ins = [a if isinstance(a, tuple) else (a, VM) for a in args]
    held = [pltpu.VMEM(shape, dtype) for shape, dtype in scratch]
    return pl.pallas_call(
        kernel,
        out_shape=[jax.ShapeDtypeStruct(o[0], o[1]) for o in outs],
        in_specs=[place for _, place in ins],
        out_specs=[o[2] if len(o) > 2 else VM for o in outs],
        scratch_shapes=held + ([pltpu.SemaphoreType.DMA((sems,))] if sems else []),
        compiler_params=pltpu.CompilerParams(vmem_limit_bytes=limit * 1024 * 1024),
        cost_estimate=pl.CostEstimate(flops=flops, bytes_accessed=2 * 10**6, transcendentals=0),
        name=name,
    )(*[a for a, _ in ins])


def exchange(rows):
    return lax.all_to_all(rows, "grid", split_axis=0, concat_axis=0, tiled=True)


def swap(block, bit):
    return lax.ppermute(block, "slide", [(i, i ^ bit) for i in range(8)])


def shards(
    embeddings,
    visible,
    window_id,
    output_gradient,
    mask_token,
    enc_qkv,
    enc_out,
    dec_qkv,
    decoder_projected,
):
    emb = embeddings[0]
    og = output_gradient[0]
    ranks = visible.reshape(16, 128)
    (send1,) = call(
        send_tokens_kernel,
        [((GROUPS * 8, 128), BF)],
        ((ranks, HERE), (emb, HERE)),
        "send_tokens",
        scratch=[((16, 128), I32), ((TILE, D), BF)],
        sems=2,
        limit=62,
    )
    recv1 = exchange(send1)
    halo = lax.ppermute(
        jnp.concatenate([emb, og], axis=1), "grid", [(i + 1, i) for i in range(GROUPS - 1)]
    )
    recv1, halo = lax.optimization_barrier((recv1, halo))
    marks, enc = call(
        plan_kernel,
        [((8, GROUPS * 8), I32), ((D, 3 * D), BF)],
        (ranks, window_id.reshape(GROUPS, TILE), enc_qkv),
        "plan",
    )
    send2, kept = call(
        encode_kernel,
        [((GROUPS * 8, 256), BF), ((4 * TOKENS, D), BF)],
        (recv1, marks, enc),
        "encode",
    )
    recv2 = exchange(send2)
    flipped, packed = call(
        prepare_kernel,
        [((4 * D, D), BF), ((PACKED, D), BF, HERE)],
        (marks, emb, og, halo, decoder_projected, enc_out, dec_qkv),
        "prepare",
        scratch=[((OG_ROWS + FRAME, D), BF)],
        sems=3,
        limit=48,
    )
    send3, keep, send = call(
        decode_kernel,
        [((GROUPS * 8, 256), BF), ((4, D, 128), BF), ((4, D, 128), BF)],
        (marks, recv2, mask_token[None, :], flipped, (packed, HERE)),
        "decode",
        scratch=[
            ((D, D), BF),
            ((D, D), BF),
            ((3 * D, D), BF),
            ((FRAME, D), BF),
            ((3 * D, FRAME), BF),
            ((D, FRAME), BF),
        ],
        sems=4,
        limit=48,
        flops=2 * 10**9,
    )
    recv3 = exchange(send3)
    sums = call(add_kernel, [((D, 128), BF)] * 4, (keep, swap(send, 1)), "add_core")
    parts = [sums[0]] + [swap(sums[j], 2 * j) for j in range(1, 4)]
    (send4,) = call(
        encode_back_kernel,
        [((GROUPS * 8, 256), BF)],
        (marks, recv3, enc_out, enc_qkv, kept, *parts),
        "encode_back",
    )
    recv4 = exchange(send4)
    tiles, grad_enc, grad_dec = call(
        finish_kernel,
        [((TILE, D), BF), ((8, 64), F32), ((8, 64), F32)],
        (marks, recv4),
        "finish",
    )
    return tiles[None], grad_enc, grad_dec


def solution(mesh):
    placed = (
        P("slide", "grid", None),
        P("slide", None),
        P("slide", None),
        P("slide", "grid", None),
        P(),
        P(),
        P(),
        P(),
        P(),
    )
    return jax.shard_map(
        shards,
        mesh=mesh,
        in_specs=placed,
        out_specs=(P("slide", "grid", None), P("grid", "slide"), P("grid", "slide")),
        check_vma=False,
    )
```

```python
import jax
import jax.numpy as jnp
from jax import lax
from jax.experimental import pallas as pl
from jax.experimental.pallas import tpu as pltpu
from jax.sharding import PartitionSpec as P

HEADS = 8
HEAD = 64
D = 512
TILE = 128
FRAME = 256
RUN = 32
GROUPS = 64
TOKENS = 32
EPS = 1e-06
SCALE = 0.125
NEG = -1e30
BF = jnp.bfloat16
F32 = jnp.float32
I32 = jnp.int32


def nn(a, b):
    return lax.dot_general(a, b, (((1,), (0,)), ((), ())), preferred_element_type=F32)


def nt(a, b):
    return lax.dot_general(a, b, (((1,), (1,)), ((), ())), preferred_element_type=F32)


def tn(a, b):
    return lax.dot_general(a, b, (((0,), (0,)), ((), ())), preferred_element_type=F32)


def iota(shape, dim):
    return lax.broadcasted_iota(I32, shape, dim)


def onehot(cond):
    return jnp.where(cond, 1.0, 0.0).astype(BF)


class Load:
    def __init__(self, source, held, sems, first, parts=1):
        self.held = held
        rows = held.shape[0] // parts
        spots = [slice(i * rows, (i + 1) * rows) for i in range(parts)]
        self.copies = [
            pltpu.make_async_copy(source.at[spot], held.at[spot], sems.at[first + i]) for i, spot in enumerate(spots)
        ]
        for copy in self.copies:
            copy.start()

    def __call__(self):
        for copy in self.copies:
            copy.wait()
        self.copies = []
        return self.held


def run_counts(visible_ref, limit):
    total = jnp.zeros(limit.shape, I32)
    for q in range(4):
        firsts = visible_ref[:, q * RUN : q * RUN + 1]
        total += jnp.sum(jnp.where(firsts < limit, 1, 0), axis=0, keepdims=True)
    return total


def frame_ranks(visible_ref, first, width):
    lane = iota((1, width), 1)
    limit = first + lane - (lane & (RUN - 1))
    seen = run_counts(visible_ref, limit)
    present = run_counts(visible_ref, limit + RUN) > seen
    return seen * RUN + (lane & (RUN - 1)), present


def own_slots(visible_ref, first):
    rank, present = frame_ranks(visible_ref, first, TILE)
    base = RUN * run_counts(visible_ref, jnp.broadcast_to(first, (1, TILE)))
    return jnp.where(present, (rank & (GROUPS - 1)) * 2 + ((rank - base) >> 6), -1)


def send_tokens_kernel(visible_hbm, emb_hbm, og_hbm, out_ref, pair_hbm, visible_b, emb_b, og_b, sems):
    visible = Load(visible_hbm, visible_b, sems, 0)
    emb = Load(emb_hbm, emb_b, sems, 1)
    og = Load(og_hbm, og_b, sems, 2)
    slot = own_slots(visible(), lax.axis_index("grid") * TILE)
    rows = iota((GROUPS * 8, TILE), 0)
    picks = [onehot(rows == slot * 4 + part) for part in range(4)]
    emb_ref = emb()
    ship_emb = pltpu.make_async_copy(emb_ref, pair_hbm.at[:, :D], sems.at[3])
    ship_emb.start()
    ship_og = pltpu.make_async_copy(og(), pair_hbm.at[:, D:], sems.at[4])
    ship_og.start()
    total = jnp.zeros((GROUPS * 8, TILE), F32)
    for part in range(4):
        total += nn(picks[part], emb_ref[:, part * 128 : (part + 1) * 128])
    out_ref[...] = total.astype(BF)
    ship_emb.wait()
    ship_og.wait()


def plan_kernel(visible_ref, wid_ref, enc_qkv_ref, mask_ref, halo_ref, marks_ref, enc_ref):
    enc_ref[...] = enc_qkv_ref[...]
    d = lax.axis_index("grid")
    first = d * TILE
    lane = iota((1, GROUPS * 8), 1)
    peer = lane >> 3
    start1 = RUN * run_counts(visible_ref, peer * TILE)
    stop1 = RUN * run_counts(visible_ref, peer * TILE + TILE)
    low1 = start1 + GROUPS * ((lane >> 2) & 1)
    marks_ref[0:1, :] = low1.astype(F32)
    marks_ref[1:2, :] = jnp.minimum(low1 + GROUPS, stop1).astype(F32)

    wid = wid_ref[...]
    last = wid[:, TILE - 1 :]
    before = jnp.concatenate([jnp.full((1, 1), -1, I32), last[:-1]], axis=0)
    more = jnp.sum(jnp.where(wid == before, 1.0, 0.0), axis=1, keepdims=True).astype(I32)
    head = iota((GROUPS, 1), 0) * TILE + more
    rows = iota((GROUPS, GROUPS * 8), 0)
    begin = jnp.sum(jnp.where(rows == peer, head, 0), axis=0, keepdims=True)
    end = jnp.sum(jnp.where(rows == peer + 1, head, 0), axis=0, keepdims=True)
    end = jnp.where(peer == GROUPS - 1, GROUPS * TILE, end)

    def visible_below(tile):
        total = jnp.zeros(tile.shape, I32)
        for q in range(4):
            firsts = visible_ref[:, q * RUN : q * RUN + 1]
            total += jnp.sum(jnp.clip(tile - firsts, 0, RUN), axis=0, keepdims=True)
        return total

    start2, stop2 = visible_below(begin), visible_below(end)
    low2 = start2 + GROUPS * ((lane >> 1) & 3)
    marks_ref[2:3, :] = low2.astype(F32)
    marks_ref[3:4, :] = jnp.minimum(low2 + GROUPS, stop2).astype(F32)
    marks_ref[4:8, :] = jnp.zeros((4, GROUPS * 8), F32)
    marks_ref[8:16, :] = jnp.broadcast_to(mask_ref[...], (8, D))

    def mine(values):
        return jnp.sum(jnp.where(lane == d * 8, values.astype(F32), 0.0), axis=1, keepdims=True).astype(I32)

    start2, stop2, begin, end = mine(start2), mine(stop2), mine(begin), mine(end)
    rank, present = frame_ranks(visible_ref, first, FRAME)
    spot = iota((1, FRAME), 1)
    live = present & (rank >= start2) & (rank < stop2)
    owned = (first + spot >= begin) & (first + spot < end)
    marks_ref[4:5, :FRAME] = jnp.where(live, (rank & (GROUPS - 1)) * 4 + ((rank - start2) >> 6), -1).astype(F32)
    marks_ref[5:6, :FRAME] = jnp.where(owned, 1.0, 0.0)
    own = wid_ref[pl.ds(d, 1), :]
    after = wid_ref[pl.ds(jnp.minimum(d + 1, GROUPS - 1), 1), :]
    marks_ref[6:7, :FRAME] = jnp.where(owned, jnp.concatenate([own, after], axis=1), -1 - spot).astype(F32)
    marks_ref[7:8, :TILE] = own_slots(visible_ref, first).astype(F32)


OUT_T, BOTH, MORE, OG_ROWS, OWN, QKV, ENC_OUT, ENC_QKV, PACKED = 1536, 0, 512, 1024, 1280, 1280, 2816, 3328, 18432


def blocks(weight_ref, out_ref, first, sems, sem):
    copies = []
    for i in range(weight_ref.shape[1] // D):
        rows = out_ref.at[first + i * D : first + (i + 1) * D]
        copies.append(pltpu.make_async_copy(weight_ref.at[:, i * D : (i + 1) * D], rows, sems.at[sem + i]))
        copies[-1].start()
    return copies


def prepare_kernel(marks_ref, emb_ref, og_ref, halo_ref, proj_ref, enc_out_ref, qkv_ref, enc_qkv_ref, flipped_ref, packed_ref, held, sems):
    copies = blocks(qkv_ref, packed_ref, QKV, sems, 0)
    copies += blocks(enc_out_ref, packed_ref, ENC_OUT, sems, 4) + blocks(enc_qkv_ref, packed_ref, ENC_QKV, sems, 5)
    flipped_ref[:OUT_T, :] = qkv_ref[...].T
    flipped_ref[OUT_T:, :] = enc_out_ref[...].T
    owned = marks_ref[5:6, :FRAME] > 0
    held[OG_ROWS : OG_ROWS + TILE, :] = og_ref[...]
    held[OG_ROWS + TILE : OG_ROWS + FRAME, :] = halo_ref[:, D:]
    og_t = jnp.concatenate([og_ref[...].T, halo_ref[:, D:].T], axis=1).astype(F32)
    og_t = jnp.where(owned, og_t, 0.0).astype(BF)
    held[BOTH:MORE, :FRAME] = nn(proj_ref[...], og_t).astype(BF)
    held[BOTH:MORE, FRAME:] = og_t
    held[MORE : MORE + D, :FRAME] = jnp.concatenate([emb_ref[...].T, halo_ref[:, :D].T], axis=1)
    across = jnp.broadcast_to(marks_ref[6:7, :FRAME], (FRAME, FRAME))
    held[MORE : MORE + FRAME, FRAME:] = jnp.where(across == across.T, 0.0, NEG).astype(BF)
    held[MORE + FRAME : MORE + D, FRAME:] = jnp.zeros((FRAME, FRAME), BF)
    copies.append(pltpu.make_async_copy(held, packed_ref.at[:OWN], sems.at[3]))
    copies[-1].start()
    for copy in copies:
        copy.wait()


def per_head(rows):
    stacked = jnp.concatenate([rows] * HEADS, axis=0)
    shape = stacked.shape
    same = iota(shape, 0) // TOKENS == iota(shape, 1) // HEAD
    return jnp.where(same, stacked.astype(F32), 0.0).astype(BF)


def fold_heads(stacked):
    shape = stacked.shape
    same = iota(shape, 0) // TOKENS == iota(shape, 1) // HEAD
    kept = jnp.where(same, stacked, 0.0)
    total = kept[:TOKENS]
    for h in range(1, HEADS):
        total += kept[h * TOKENS : (h + 1) * TOKENS]
    return total


def group_match(marks_ref, row):
    ranks = iota((TOKENS, GROUPS * 8), 0) * GROUPS + lax.axis_index("grid")
    low, high = marks_ref[row : row + 1, :].astype(I32), marks_ref[row + 1 : row + 2, :].astype(I32)
    return (ranks >= low) & (ranks < high)


def encoder_probs(queries, keys):
    scores = nt(per_head(queries), keys) * SCALE
    weights = jnp.exp(scores - jnp.max(scores, axis=1, keepdims=True))
    return weights / jnp.sum(weights, axis=1, keepdims=True)


def encode_kernel(recv_ref, marks_ref, weight_ref, out_ref, store, kept_ref, sems):
    match1 = group_match(marks_ref, 0)
    lanes = iota((TOKENS, GROUPS * 8), 1)
    recv = recv_ref[...]
    x = jnp.concatenate([nn(onehot(match1 & (lanes % 4 == part)), recv) for part in range(4)], axis=1)
    kept_ref[:TOKENS, :] = x.astype(BF)
    normed = (x * lax.rsqrt(jnp.mean(x * x, axis=1, keepdims=True) + EPS)).astype(BF)
    qkv = nn(normed, weight_ref[...]).astype(BF)
    for i in range(3):
        kept_ref[(i + 1) * TOKENS : (i + 2) * TOKENS, :] = qkv[:, i * D : (i + 1) * D]
    keep = pltpu.make_async_copy(kept_ref, store.at[: 4 * TOKENS], sems.at[0])
    keep.start()
    soft = encoder_probs(qkv[:, :D], qkv[:, D : 2 * D])
    context = fold_heads(nn(soft.astype(BF), qkv[:, 2 * D :])).astype(BF)
    match2 = group_match(marks_ref, 2)
    out = tn(onehot(match2 & (lanes % 2 == 0)), context[:, :256])
    out += tn(onehot(match2 & (lanes % 2 == 1)), context[:, 256:])
    out_ref[...] = out.astype(BF)
    keep.wait()


def decode_kernel(marks_ref, recv_ref, flipped_ref, packed, out_hbm, keep_ref, send_ref, out_ref, more_b, both_b, qkv_b, og_b, dqkv_ref, ctx_ref, sems):
    more = Load(packed.at[MORE:OG_ROWS], more_b, sems, 0)
    both = Load(packed.at[BOTH:MORE], both_b, sems, 1)
    qkv_w = Load(packed.at[QKV : QKV + 3 * D], qkv_b, sems, 2)
    og_rows = Load(packed.at[OG_ROWS:OWN], og_b, sems, 3)
    slot = marks_ref[4:5, :FRAME].astype(I32)
    live = slot >= 0
    owned = marks_ref[5:6, :FRAME] > 0
    blank = jnp.broadcast_to(marks_ref[8:9, :], (TILE, D)).T[:, :1]
    rows = iota((GROUPS * 8, FRAME), 0)
    pick = [onehot(rows == slot * 2 + half) for half in range(2)]
    recv = recv_ref[...]
    ctx_enc = jnp.concatenate([tn(recv, pick[half]) for half in range(2)], axis=0).astype(BF)
    delta = nn(flipped_ref[OUT_T:, :], ctx_enc)
    x = jnp.where(live, (more()[:, :FRAME].astype(F32) + delta).astype(BF).astype(F32), blank)
    inv = lax.rsqrt(jnp.mean(x * x, axis=0, keepdims=True) + EPS)
    normed = (x * inv).astype(BF)
    qkv = nn(flipped_ref[:OUT_T, :], normed).astype(BF)
    keys = qkv[D : 2 * D].T
    vals = qkv[2 * D :].T
    bias_rows = more()[:FRAME, FRAME:].astype(F32)
    both_b = both()
    for h in range(HEADS):
        spot = slice(h * HEAD, (h + 1) * HEAD)
        q_t, k_t, v_t = qkv[spot], qkv[D + h * HEAD : D + (h + 1) * HEAD], qkv[2 * D + h * HEAD : 2 * D + (h + 1) * HEAD]
        d_t = both_b[spot, :FRAME]
        scores = nn(keys[:, spot], q_t) * SCALE + bias_rows
        weights = jnp.exp(scores - jnp.max(scores, axis=0, keepdims=True))
        probs = weights * (1.0 / jnp.sum(weights, axis=0, keepdims=True))
        probs_b = probs.astype(BF)
        ctx_ref[spot, :] = jnp.where(owned, nn(v_t, probs_b), 0.0).astype(BF)
        dprobs = nn(vals[:, spot], d_t).astype(BF).astype(F32)
        inner = jnp.sum(probs * dprobs, axis=0, keepdims=True)
        dscores = (probs * (dprobs - inner) * SCALE).astype(BF)
        dqkv_ref[spot, :] = nn(k_t, dscores).astype(BF)
        dqkv_ref[D + h * HEAD : D + (h + 1) * HEAD, :] = nt(q_t, dscores).astype(BF)
        dqkv_ref[2 * D + h * HEAD : 2 * D + (h + 1) * HEAD, :] = nt(d_t, probs_b).astype(BF)

    weight_ref = qkv_w()
    dnormed = nn(weight_ref[:D, :], dqkv_ref[:D, :])
    for i in range(1, 3):
        dnormed += nn(weight_ref[i * D : (i + 1) * D, :], dqkv_ref[i * D : (i + 1) * D, :])
    slope = inv * inv * inv * jnp.mean(x * dnormed, axis=0, keepdims=True)
    dx = (inv * dnormed - x * slope + both_b[:, FRAME:].astype(F32)).astype(BF)
    dx_rows = dx.T
    out = nn(pick[0], dx_rows[:, :256]) + nn(pick[1], dx_rows[:, 256:])
    out_ref[...] = out.astype(BF)
    ship = pltpu.make_async_copy(out_ref, out_hbm, sems.at[4])
    ship.start()

    me = lax.axis_index("slide")
    even = (me & 1) == 0
    grad_enc = nn(ctx_enc, dx_rows).astype(BF)
    grad_dec = nn(ctx_ref[...], og_rows()[...]).astype(BF)

    def block(s):
        spot = slice(s * 64, (s + 1) * 64)
        return jnp.concatenate([grad_enc[:, spot], grad_dec[:, spot]], axis=1)

    for m in range(4):
        low, high = block(2 * m), block(2 * m + 1)
        j = m ^ (me >> 1)
        keep_ref[j] = jnp.where(even, low, high)
        send_ref[j] = jnp.where(even, high, low)
    ship.wait()


def add_kernel(keep_ref, recv_ref, *outs):
    for j in range(4):
        outs[j][...] = (keep_ref[j].astype(F32) + recv_ref[j].astype(F32)).astype(BF)


def encode_back_kernel(marks_ref, recv_ref, packed, store, out_ref, enc_out_b, kept_b, weight_b, sems):
    enc_out = Load(packed.at[ENC_OUT:ENC_QKV], enc_out_b, sems, 0, 2)
    kept = Load(store.at[: 4 * TOKENS], kept_b, sems, 2)
    weight = Load(packed.at[ENC_QKV : ENC_QKV + 3 * D], weight_b, sems, 3, 3)
    match2 = group_match(marks_ref, 2)
    lanes = iota((TOKENS, GROUPS * 8), 1)
    recv = recv_ref[...]
    grad = jnp.concatenate(
        [nn(onehot(match2 & (lanes % 2 == half)), recv) for half in range(2)], axis=1
    )
    dctx = per_head(nt(grad.astype(BF), enc_out()[...]).astype(BF))
    kept_ref = kept()
    queries, keys, values = [kept_ref[i * TOKENS : (i + 1) * TOKENS, :] for i in range(1, 4)]
    probs = encoder_probs(queries, keys)
    dprobs = nt(dctx, values).astype(BF).astype(F32)
    inner = jnp.sum(probs * dprobs, axis=1, keepdims=True)
    dscores = (probs * (dprobs - inner) * SCALE).astype(BF)
    dq = fold_heads(nn(dscores, keys))
    dk = tn(dscores, per_head(queries))
    dv = tn(probs.astype(BF), dctx)
    weight_ref = weight()
    dnormed = nt(dq.astype(BF), weight_ref[:D, :])
    dnormed += nt(dk.astype(BF), weight_ref[D : 2 * D, :])
    dnormed += nt(dv.astype(BF), weight_ref[2 * D :, :])
    dnormed = dnormed.astype(BF).astype(F32)
    x = kept_ref[:TOKENS, :].astype(F32)
    inv = lax.rsqrt(jnp.mean(x * x, axis=1, keepdims=True) + EPS)
    slope = inv * inv * inv * jnp.mean(x * dnormed, axis=1, keepdims=True)
    dtokens = (grad + (inv * dnormed - x * slope)).astype(BF)
    match1 = group_match(marks_ref, 0)
    out = jnp.zeros((GROUPS * 8, 128), F32)
    for part in range(4):
        out += tn(onehot(match1 & (lanes % 4 == part)), dtokens[:, part * 128 : (part + 1) * 128])
    out_ref[...] = out.astype(BF)


def join_kernel(tokens_ref, part0, part1, part2, part3, out_ref):
    out_ref[:, :128] = tokens_ref[...]
    parts = [p[...].astype(F32) for p in (part0, part1, part2, part3)]
    out_ref[:, 128:] = (parts[0] + parts[1] + parts[2] + parts[3]).astype(BF)


def finish_kernel(marks_ref, recv_ref, tiles_ref, enc_ref, dec_ref):
    slot = jnp.broadcast_to(marks_ref[7:8, :TILE], (TILE, TILE)).T[:, 0:1].astype(I32)
    lanes = iota((TILE, GROUPS * 8), 1)
    recv = recv_ref[:, :128]
    for part in range(4):
        tiles_ref[:, part * 128 : (part + 1) * 128] = nn(onehot(lanes == slot * 4 + part), recv).astype(BF)
    rows = recv_ref[:, 128:].astype(F32).reshape(GROUPS, 8, 128)
    total = jnp.sum(rows, axis=0)
    enc_ref[...] = total[:, :64]
    dec_ref[...] = total[:, 64:]


VM = pl.BlockSpec(memory_space=pltpu.VMEM)
HERE = pl.BlockSpec(memory_space=pl.ANY)


def call(kernel, outs, args, name, scratch=(), limit=16, flops=10**8, sems=0):
    ins = [a if isinstance(a, tuple) else (a, VM) for a in args]
    held = [pltpu.VMEM(shape, dtype) for shape, dtype in scratch]
    return pl.pallas_call(
        kernel,
        out_shape=[jax.ShapeDtypeStruct(o[0], o[1]) for o in outs],
        in_specs=[place for _, place in ins],
        out_specs=[o[2] if len(o) > 2 else VM for o in outs],
        scratch_shapes=held + ([pltpu.SemaphoreType.DMA((sems,))] if sems else []),
        compiler_params=pltpu.CompilerParams(vmem_limit_bytes=limit * 1024 * 1024),
        cost_estimate=pl.CostEstimate(flops=flops, bytes_accessed=2 * 10**6, transcendentals=0),
        name=name,
    )(*[a for a, _ in ins])


def exchange(rows):
    return lax.all_to_all(rows, "grid", split_axis=0, concat_axis=0, tiled=True)


def swap(block, bit):
    return lax.ppermute(block, "slide", [(i, i ^ bit) for i in range(8)])


def shards(
    embeddings,
    visible,
    window_id,
    output_gradient,
    mask_token,
    enc_qkv,
    enc_out,
    dec_qkv,
    decoder_projected,
):
    emb = embeddings[0]
    og = output_gradient[0]
    ranks = visible.reshape(16, 128)
    send1, pair = call(
        send_tokens_kernel,
        [((GROUPS * 8, 128), BF), ((TILE, 2 * D), BF, HERE)],
        ((ranks, HERE), (emb, HERE), (og, HERE)),
        "send_tokens",
        scratch=[((16, 128), I32), ((TILE, D), BF), ((TILE, D), BF)],
        sems=5,
        limit=62,
    )
    halo = lax.ppermute(pair, "grid", [(i + 1, i) for i in range(GROUPS - 1)])
    recv1 = exchange(send1)
    marks, enc = call(
        plan_kernel,
        [((16, GROUPS * 8), F32), ((D, 3 * D), BF)],
        (ranks, window_id.reshape(GROUPS, TILE), enc_qkv, mask_token[None, :], (halo, HERE)),
        "plan",
        flops=4 * 10**9,
    )
    send2, kept = call(
        encode_kernel,
        [((GROUPS * 8, 256), BF), ((PACKED, D), BF, HERE)],
        (recv1, marks, enc),
        "encode",
        scratch=[((4 * TOKENS, D), BF)],
        sems=1,
        limit=40,
    )
    recv2 = exchange(send2)
    flipped, packed = call(
        prepare_kernel,
        [((4 * D, D), BF), ((PACKED, D), BF, HERE)],
        (marks, emb, og, halo, decoder_projected, enc_out, dec_qkv, enc_qkv),
        "prepare",
        scratch=[((OWN, D), BF)],
        sems=8,
        limit=40,
    )
    send3, keep, send = call(
        decode_kernel,
        [((GROUPS * 8, 256), BF, HERE), ((4, D, 128), BF), ((4, D, 128), BF)],
        (marks, recv2, flipped, (packed, HERE)),
        "decode",
        scratch=[
            ((GROUPS * 8, 256), BF),
            ((D, D), BF),
            ((D, D), BF),
            ((3 * D, D), BF),
            ((FRAME, D), BF),
            ((3 * D, FRAME), BF),
            ((D, FRAME), BF),
        ],
        sems=5,
        limit=48,
        flops=2 * 10**9,
    )
    recv3 = exchange(send3)
    sums = call(add_kernel, [((D, 128), BF)] * 4, (keep, swap(send, 1)), "add_core")
    parts = [sums[0]] + [swap(sums[j], 2 * j) for j in range(1, 4)]
    (back,) = call(
        encode_back_kernel,
        [((GROUPS * 8, 128), BF)],
        (marks, recv3, (packed, HERE), (kept, HERE)),
        "encode_back",
        scratch=[((D, D), BF), ((4 * TOKENS, D), BF), ((3 * D, D), BF)],
        sems=6,
        limit=48,
        flops=2 * 10**9,
    )
    (send4,) = call(join_kernel, [((GROUPS * 8, 256), BF)], (back, *parts), "join")
    recv4 = exchange(send4)
    tiles, grad_enc, grad_dec = call(
        finish_kernel,
        [((TILE, D), BF), ((8, 64), F32), ((8, 64), F32)],
        (marks, recv4),
        "finish",
    )
    return tiles[None], grad_enc, grad_dec


def solution(mesh):
    placed = (
        P("slide", "grid", None),
        P("slide", None),
        P("slide", None),
        P("slide", "grid", None),
        P(),
        P(),
        P(),
        P(),
        P(),
    )
    return jax.shard_map(
        shards,
        mesh=mesh,
        in_specs=placed,
        out_specs=(P("slide", "grid", None), P("grid", "slide"), P("grid", "slide")),
        check_vma=False,
    )
```

```python
import jax
import jax.numpy as jnp
from jax import lax
from jax.experimental import pallas as pl
from jax.experimental.pallas import tpu as pltpu
from jax.sharding import PartitionSpec as P

HEADS = 8
HEAD = 64
D = 512
TILE = 128
FRAME = 256
RUN = 32
GROUPS = 64
TOKENS = 32
EPS = 1e-06
SCALE = 0.125
LOG2E = 1.4426950408889634
NEG = -1e30
BF = jnp.bfloat16
F32 = jnp.float32
I32 = jnp.int32


def nn(a, b):
    return lax.dot_general(a, b, (((1,), (0,)), ((), ())), preferred_element_type=F32)


def nt(a, b):
    return lax.dot_general(a, b, (((1,), (1,)), ((), ())), preferred_element_type=F32)


def tn(a, b):
    return lax.dot_general(a, b, (((0,), (0,)), ((), ())), preferred_element_type=F32)


def iota(shape, dim):
    return lax.broadcasted_iota(I32, shape, dim)


def onehot(cond):
    return jnp.where(cond, 1.0, 0.0).astype(BF)


class Load:
    def __init__(self, source, held, sems, first, parts=1):
        self.held = held
        rows = held.shape[0] // parts
        spots = [slice(i * rows, (i + 1) * rows) for i in range(parts)]
        self.copies = [
            pltpu.make_async_copy(source.at[spot], held.at[spot], sems.at[first + i]) for i, spot in enumerate(spots)
        ]
        for copy in self.copies:
            copy.start()

    def __call__(self):
        for copy in self.copies:
            copy.wait()
        self.copies = []
        return self.held


def run_counts(visible_ref, limit):
    total = jnp.zeros(limit.shape, I32)
    for q in range(4):
        firsts = visible_ref[:, q * RUN : q * RUN + 1]
        total += jnp.sum(jnp.where(firsts < limit, 1, 0), axis=0, keepdims=True)
    return total


def frame_ranks(visible_ref, first, width):
    lane = iota((1, width), 1)
    limit = first + lane - (lane & (RUN - 1))
    seen = run_counts(visible_ref, limit)
    present = run_counts(visible_ref, limit + RUN) > seen
    return seen * RUN + (lane & (RUN - 1)), present


def own_slots(visible_ref, first):
    rank, present = frame_ranks(visible_ref, first, TILE)
    base = RUN * run_counts(visible_ref, jnp.broadcast_to(first, (1, TILE)))
    return jnp.where(present, (rank & (GROUPS - 1)) * 2 + ((rank - base) >> 6), -1)


def send_tokens_kernel(visible_hbm, emb_hbm, og_hbm, out_ref, pair_hbm, visible_b, emb_b, og_b, sems):
    visible = Load(visible_hbm, visible_b, sems, 0)
    emb = Load(emb_hbm, emb_b, sems, 1)
    og = Load(og_hbm, og_b, sems, 2)
    slot = own_slots(visible(), lax.axis_index("grid") * TILE)
    rows = iota((GROUPS * 8, TILE), 0)
    picks = [onehot(rows == slot * 4 + part) for part in range(4)]
    emb_ref = emb()
    ship_emb = pltpu.make_async_copy(emb_ref, pair_hbm.at[:, :D], sems.at[3])
    ship_emb.start()
    ship_og = pltpu.make_async_copy(og(), pair_hbm.at[:, D:], sems.at[4])
    ship_og.start()
    total = jnp.zeros((GROUPS * 8, TILE), F32)
    for part in range(4):
        total += nn(picks[part], emb_ref[:, part * 128 : (part + 1) * 128])
    out_ref[...] = total.astype(BF)
    ship_emb.wait()
    ship_og.wait()


def plan_kernel(visible_ref, wid_ref, enc_qkv_ref, mask_ref, halo_ref, marks_ref, enc_ref):
    enc_ref[...] = enc_qkv_ref[...]
    d = lax.axis_index("grid")
    first = d * TILE
    lane = iota((1, GROUPS * 8), 1)
    peer = lane >> 3
    start1 = RUN * run_counts(visible_ref, peer * TILE)
    stop1 = RUN * run_counts(visible_ref, peer * TILE + TILE)
    low1 = start1 + GROUPS * ((lane >> 2) & 1)
    marks_ref[0:1, :] = low1.astype(F32)
    marks_ref[1:2, :] = jnp.minimum(low1 + GROUPS, stop1).astype(F32)

    wid = wid_ref[...]
    last = wid[:, TILE - 1 :]
    before = jnp.concatenate([jnp.full((1, 1), -1, I32), last[:-1]], axis=0)
    more = jnp.sum(jnp.where(wid == before, 1.0, 0.0), axis=1, keepdims=True).astype(I32)
    head = iota((GROUPS, 1), 0) * TILE + more
    rows = iota((GROUPS, GROUPS * 8), 0)
    begin = jnp.sum(jnp.where(rows == peer, head, 0), axis=0, keepdims=True)
    end = jnp.sum(jnp.where(rows == peer + 1, head, 0), axis=0, keepdims=True)
    end = jnp.where(peer == GROUPS - 1, GROUPS * TILE, end)

    def visible_below(tile):
        total = jnp.zeros(tile.shape, I32)
        for q in range(4):
            firsts = visible_ref[:, q * RUN : q * RUN + 1]
            total += jnp.sum(jnp.clip(tile - firsts, 0, RUN), axis=0, keepdims=True)
        return total

    start2, stop2 = visible_below(begin), visible_below(end)
    low2 = start2 + GROUPS * ((lane >> 1) & 3)
    marks_ref[2:3, :] = low2.astype(F32)
    marks_ref[3:4, :] = jnp.minimum(low2 + GROUPS, stop2).astype(F32)
    marks_ref[4:8, :] = jnp.zeros((4, GROUPS * 8), F32)
    marks_ref[8:16, :] = jnp.broadcast_to(mask_ref[...], (8, D))

    def mine(values):
        return jnp.sum(jnp.where(lane == d * 8, values.astype(F32), 0.0), axis=1, keepdims=True).astype(I32)

    start2, stop2, begin, end = mine(start2), mine(stop2), mine(begin), mine(end)
    rank, present = frame_ranks(visible_ref, first, FRAME)
    spot = iota((1, FRAME), 1)
    live = present & (rank >= start2) & (rank < stop2)
    owned = (first + spot >= begin) & (first + spot < end)
    marks_ref[4:5, :FRAME] = jnp.where(live, (rank & (GROUPS - 1)) * 4 + ((rank - start2) >> 6), -1).astype(F32)
    marks_ref[5:6, :FRAME] = jnp.where(owned, 1.0, 0.0)
    own = wid_ref[pl.ds(d, 1), :]
    after = wid_ref[pl.ds(jnp.minimum(d + 1, GROUPS - 1), 1), :]
    marks_ref[6:7, :FRAME] = jnp.where(owned, jnp.concatenate([own, after], axis=1), -1 - spot).astype(F32)
    marks_ref[7:8, :TILE] = own_slots(visible_ref, first).astype(F32)


OUT_T, BOTH, MORE, OG_ROWS, OWN, QKV, ENC_OUT, ENC_QKV, PACKED = 1536, 0, 512, 1024, 1280, 1280, 2816, 3328, 18432


def blocks(weight_ref, out_ref, first, sems, sem):
    copies = []
    for i in range(weight_ref.shape[1] // D):
        rows = out_ref.at[first + i * D : first + (i + 1) * D]
        copies.append(pltpu.make_async_copy(weight_ref.at[:, i * D : (i + 1) * D], rows, sems.at[sem + i]))
        copies[-1].start()
    return copies


def prepare_kernel(marks_ref, emb_ref, og_ref, halo_ref, proj_ref, enc_out_ref, qkv_ref, enc_qkv_ref, flipped_ref, packed_ref, held, sems):
    copies = blocks(qkv_ref, packed_ref, QKV, sems, 0)
    copies += blocks(enc_out_ref, packed_ref, ENC_OUT, sems, 4) + blocks(enc_qkv_ref, packed_ref, ENC_QKV, sems, 5)
    flipped_ref[:OUT_T, :] = qkv_ref[...].T
    flipped_ref[OUT_T:, :] = enc_out_ref[...].T
    owned = marks_ref[5:6, :FRAME] > 0
    held[OG_ROWS : OG_ROWS + TILE, :] = og_ref[...]
    held[OG_ROWS + TILE : OG_ROWS + FRAME, :] = halo_ref[:, D:]
    og_t = jnp.concatenate([og_ref[...].T, halo_ref[:, D:].T], axis=1).astype(F32)
    og_t = jnp.where(owned, og_t, 0.0).astype(BF)
    held[BOTH:MORE, :FRAME] = nn(proj_ref[...], og_t).astype(BF)
    held[BOTH:MORE, FRAME:] = og_t
    held[MORE : MORE + D, :FRAME] = jnp.concatenate([emb_ref[...].T, halo_ref[:, :D].T], axis=1)
    across = jnp.broadcast_to(marks_ref[6:7, :FRAME], (FRAME, FRAME))
    held[MORE : MORE + FRAME, FRAME:] = jnp.where(across == across.T, 0.0, NEG).astype(BF)
    held[MORE + FRAME : MORE + D, FRAME:] = jnp.zeros((FRAME, FRAME), BF)
    copies.append(pltpu.make_async_copy(held, packed_ref.at[:OWN], sems.at[3]))
    copies[-1].start()
    for copy in copies:
        copy.wait()


def per_head(rows):
    stacked = jnp.concatenate([rows] * HEADS, axis=0)
    shape = stacked.shape
    same = iota(shape, 0) // TOKENS == iota(shape, 1) // HEAD
    return jnp.where(same, stacked.astype(F32), 0.0).astype(BF)


def fold_heads(stacked):
    shape = stacked.shape
    same = iota(shape, 0) // TOKENS == iota(shape, 1) // HEAD
    kept = jnp.where(same, stacked, 0.0)
    total = kept[:TOKENS]
    for h in range(1, HEADS):
        total += kept[h * TOKENS : (h + 1) * TOKENS]
    return total


def group_match(marks_ref, row):
    ranks = iota((TOKENS, GROUPS * 8), 0) * GROUPS + lax.axis_index("grid")
    low, high = marks_ref[row : row + 1, :].astype(I32), marks_ref[row + 1 : row + 2, :].astype(I32)
    return (ranks >= low) & (ranks < high)


def encoder_probs(queries, keys):
    scores = nt(per_head(queries), keys) * SCALE
    weights = jnp.exp(scores - jnp.max(scores, axis=1, keepdims=True))
    return weights / jnp.sum(weights, axis=1, keepdims=True)


def encode_kernel(recv_ref, marks_ref, weight_ref, out_ref, store, kept_ref, sems):
    match1 = group_match(marks_ref, 0)
    lanes = iota((TOKENS, GROUPS * 8), 1)
    recv = recv_ref[...]
    x = jnp.concatenate([nn(onehot(match1 & (lanes % 4 == part)), recv) for part in range(4)], axis=1)
    kept_ref[:TOKENS, :] = x.astype(BF)
    normed = (x * lax.rsqrt(jnp.mean(x * x, axis=1, keepdims=True) + EPS)).astype(BF)
    qkv = nn(normed, weight_ref[...]).astype(BF)
    for i in range(3):
        kept_ref[(i + 1) * TOKENS : (i + 2) * TOKENS, :] = qkv[:, i * D : (i + 1) * D]
    keep = pltpu.make_async_copy(kept_ref, store.at[: 4 * TOKENS], sems.at[0])
    keep.start()
    soft = encoder_probs(qkv[:, :D], qkv[:, D : 2 * D])
    context = fold_heads(nn(soft.astype(BF), qkv[:, 2 * D :])).astype(BF)
    match2 = group_match(marks_ref, 2)
    out = tn(onehot(match2 & (lanes % 2 == 0)), context[:, :256])
    out += tn(onehot(match2 & (lanes % 2 == 1)), context[:, 256:])
    out_ref[...] = out.astype(BF)
    keep.wait()


def decode_kernel(marks_ref, recv_ref, flipped_ref, packed, out_hbm, keep_ref, send_ref, out_ref, more_b, both_b, qkv_b, og_b, dqkv_ref, ctx_ref, sems):
    more = Load(packed.at[MORE:OG_ROWS], more_b, sems, 0)
    both = Load(packed.at[BOTH:MORE], both_b, sems, 1)
    qkv_w = Load(packed.at[QKV : QKV + 3 * D], qkv_b, sems, 2)
    og_rows = Load(packed.at[OG_ROWS:OWN], og_b, sems, 3)
    slot = marks_ref[4:5, :FRAME].astype(I32)
    live = slot >= 0
    owned = marks_ref[5:6, :FRAME] > 0
    blank = jnp.broadcast_to(marks_ref[8:9, :], (TILE, D)).T[:, :1]
    rows = iota((GROUPS * 8, FRAME), 0)
    pick = [onehot(rows == slot * 2 + half) for half in range(2)]
    recv = recv_ref[...]
    ctx_enc = jnp.concatenate([tn(recv, pick[half]) for half in range(2)], axis=0).astype(BF)
    delta = nn(flipped_ref[OUT_T:, :], ctx_enc)
    x = jnp.where(live, (more()[:, :FRAME].astype(F32) + delta).astype(BF).astype(F32), blank)
    inv = lax.rsqrt(jnp.mean(x * x, axis=0, keepdims=True) + EPS)
    normed = (x * inv).astype(BF)
    keys_t = nn(flipped_ref[D : 2 * D, :], normed).astype(BF)
    keys = keys_t.T
    vals_t = nn(flipped_ref[2 * D : OUT_T, :], normed).astype(BF)
    vals = vals_t.T
    qkv = (nn(flipped_ref[:D, :], normed).astype(BF), keys_t, vals_t)
    bias_rows = more()[:FRAME, FRAME:].astype(F32)
    both_b = both()
    for first in range(0, HEADS, 8):
        group = range(first, first + 8)
        q, k, v, d = {}, {}, {}, {}
        for h in group:
            spot = slice(h * HEAD, (h + 1) * HEAD)
            q[h], k[h], v[h] = [block[spot] for block in qkv]
            d[h] = both_b[spot, :FRAME]
        scores = {h: nn(keys[:, h * HEAD : (h + 1) * HEAD], q[h]) for h in group}
        dprobs = {h: nn(vals[:, h * HEAD : (h + 1) * HEAD], d[h]) for h in group}
        probs = {}
        for h in group:
            logits = scores[h] * (SCALE * LOG2E) + bias_rows
            weights = jnp.exp2(logits - jnp.max(logits, axis=0, keepdims=True))
            probs[h] = weights * (1.0 / jnp.sum(weights, axis=0, keepdims=True))
        probs_b = {h: probs[h].astype(BF) for h in group}
        context = {h: nn(v[h], probs_b[h]) for h in group}
        dscores = {}
        for h in group:
            ctx_ref[h * HEAD : (h + 1) * HEAD, :] = jnp.where(owned, context[h], 0.0).astype(BF)
            inner = jnp.sum(context[h] * d[h].astype(F32), axis=0, keepdims=True)
            dscores[h] = (probs[h] * (dprobs[h] - inner)).astype(BF)
        for h in group:
            dqkv_ref[h * HEAD : (h + 1) * HEAD, :] = (nn(k[h], dscores[h]) * SCALE).astype(BF)
            dqkv_ref[D + h * HEAD : D + (h + 1) * HEAD, :] = (nt(q[h], dscores[h]) * SCALE).astype(BF)
            dqkv_ref[2 * D + h * HEAD : 2 * D + (h + 1) * HEAD, :] = nt(d[h], probs_b[h]).astype(BF)

    weight_ref = qkv_w()
    dnormed = nn(weight_ref[:D, :], dqkv_ref[:D, :])
    for i in range(1, 3):
        dnormed += nn(weight_ref[i * D : (i + 1) * D, :], dqkv_ref[i * D : (i + 1) * D, :])
    slope = inv * inv * inv * jnp.mean(x * dnormed, axis=0, keepdims=True)
    dx = (inv * dnormed - x * slope + both_b[:, FRAME:].astype(F32)).astype(BF)
    dx_rows = dx.T
    out = nn(pick[0], dx_rows[:, :256]) + nn(pick[1], dx_rows[:, 256:])
    out_ref[...] = out.astype(BF)
    ship = pltpu.make_async_copy(out_ref, out_hbm, sems.at[4])
    ship.start()

    me = lax.axis_index("slide")
    even = (me & 1) == 0
    grad_enc = nn(ctx_enc, dx_rows).astype(BF)
    grad_dec = nn(ctx_ref[...], og_rows()[...]).astype(BF)

    def block(s):
        spot = slice(s * 64, (s + 1) * 64)
        return jnp.concatenate([grad_enc[:, spot], grad_dec[:, spot]], axis=1)

    for m in range(4):
        low, high = block(2 * m), block(2 * m + 1)
        j = m ^ (me >> 1)
        keep_ref[j] = jnp.where(even, low, high)
        send_ref[j] = jnp.where(even, high, low)
    ship.wait()


def add_kernel(keep_ref, recv_ref, *outs):
    for j in range(4):
        outs[j][...] = (keep_ref[j].astype(F32) + recv_ref[j].astype(F32)).astype(BF)


def encode_back_kernel(marks_ref, recv_ref, packed, store, out_ref, enc_out_b, kept_b, weight_b, sems):
    enc_out = Load(packed.at[ENC_OUT:ENC_QKV], enc_out_b, sems, 0, 2)
    kept = Load(store.at[: 4 * TOKENS], kept_b, sems, 2)
    weight = Load(packed.at[ENC_QKV : ENC_QKV + 3 * D], weight_b, sems, 3, 3)
    match2 = group_match(marks_ref, 2)
    lanes = iota((TOKENS, GROUPS * 8), 1)
    recv = recv_ref[...]
    grad = jnp.concatenate(
        [nn(onehot(match2 & (lanes % 2 == half)), recv) for half in range(2)], axis=1
    )
    dctx = per_head(nt(grad.astype(BF), enc_out()[...]).astype(BF))
    kept_ref = kept()
    queries, keys, values = [kept_ref[i * TOKENS : (i + 1) * TOKENS, :] for i in range(1, 4)]
    probs = encoder_probs(queries, keys)
    dprobs = nt(dctx, values).astype(BF).astype(F32)
    inner = jnp.sum(probs * dprobs, axis=1, keepdims=True)
    dscores = (probs * (dprobs - inner) * SCALE).astype(BF)
    dq = fold_heads(nn(dscores, keys))
    dk = tn(dscores, per_head(queries))
    dv = tn(probs.astype(BF), dctx)
    weight_ref = weight()
    dnormed = nt(dq.astype(BF), weight_ref[:D, :])
    dnormed += nt(dk.astype(BF), weight_ref[D : 2 * D, :])
    dnormed += nt(dv.astype(BF), weight_ref[2 * D :, :])
    dnormed = dnormed.astype(BF).astype(F32)
    x = kept_ref[:TOKENS, :].astype(F32)
    inv = lax.rsqrt(jnp.mean(x * x, axis=1, keepdims=True) + EPS)
    slope = inv * inv * inv * jnp.mean(x * dnormed, axis=1, keepdims=True)
    dtokens = (grad + (inv * dnormed - x * slope)).astype(BF)
    match1 = group_match(marks_ref, 0)
    out = jnp.zeros((GROUPS * 8, 128), F32)
    for part in range(4):
        out += tn(onehot(match1 & (lanes % 4 == part)), dtokens[:, part * 128 : (part + 1) * 128])
    out_ref[...] = out.astype(BF)


def join_kernel(tokens_ref, part0, part1, part2, part3, out_ref):
    out_ref[:, :128] = tokens_ref[...]
    parts = [p[...].astype(F32) for p in (part0, part1, part2, part3)]
    out_ref[:, 128:] = (parts[0] + parts[1] + parts[2] + parts[3]).astype(BF)


def finish_kernel(marks_ref, recv_ref, tiles_ref, enc_ref, dec_ref):
    slot = jnp.broadcast_to(marks_ref[7:8, :TILE], (TILE, TILE)).T[:, 0:1].astype(I32)
    lanes = iota((TILE, GROUPS * 8), 1)
    recv = recv_ref[:, :128]
    for part in range(4):
        tiles_ref[:, part * 128 : (part + 1) * 128] = nn(onehot(lanes == slot * 4 + part), recv).astype(BF)
    rows = recv_ref[:, 128:].astype(F32).reshape(GROUPS, 8, 128)
    total = jnp.sum(rows, axis=0)
    enc_ref[...] = total[:, :64]
    dec_ref[...] = total[:, 64:]


VM = pl.BlockSpec(memory_space=pltpu.VMEM)
HERE = pl.BlockSpec(memory_space=pl.ANY)


def call(kernel, outs, args, name, scratch=(), limit=16, flops=10**8, sems=0):
    ins = [a if isinstance(a, tuple) else (a, VM) for a in args]
    held = [pltpu.VMEM(shape, dtype) for shape, dtype in scratch]
    return pl.pallas_call(
        kernel,
        out_shape=[jax.ShapeDtypeStruct(o[0], o[1]) for o in outs],
        in_specs=[place for _, place in ins],
        out_specs=[o[2] if len(o) > 2 else VM for o in outs],
        scratch_shapes=held + ([pltpu.SemaphoreType.DMA((sems,))] if sems else []),
        compiler_params=pltpu.CompilerParams(vmem_limit_bytes=limit * 1024 * 1024),
        cost_estimate=pl.CostEstimate(flops=flops, bytes_accessed=2 * 10**6, transcendentals=0),
        name=name,
    )(*[a for a, _ in ins])


def exchange(rows):
    return lax.all_to_all(rows, "grid", split_axis=0, concat_axis=0, tiled=True)


def swap(block, bit):
    return lax.ppermute(block, "slide", [(i, i ^ bit) for i in range(8)])


def shards(
    embeddings,
    visible,
    window_id,
    output_gradient,
    mask_token,
    enc_qkv,
    enc_out,
    dec_qkv,
    decoder_projected,
):
    emb = embeddings[0]
    og = output_gradient[0]
    ranks = visible.reshape(16, 128)
    send1, pair = call(
        send_tokens_kernel,
        [((GROUPS * 8, 128), BF), ((TILE, 2 * D), BF, HERE)],
        ((ranks, HERE), (emb, HERE), (og, HERE)),
        "send_tokens",
        scratch=[((16, 128), I32), ((TILE, D), BF), ((TILE, D), BF)],
        sems=5,
        limit=62,
    )
    halo = lax.ppermute(pair, "grid", [(i + 1, i) for i in range(GROUPS - 1)])
    recv1 = exchange(send1)
    marks, enc = call(
        plan_kernel,
        [((16, GROUPS * 8), F32), ((D, 3 * D), BF)],
        (ranks, window_id.reshape(GROUPS, TILE), enc_qkv, mask_token[None, :], (halo, HERE)),
        "plan",
        flops=4 * 10**9,
    )
    send2, kept = call(
        encode_kernel,
        [((GROUPS * 8, 256), BF), ((PACKED, D), BF, HERE)],
        (recv1, marks, enc),
        "encode",
        scratch=[((4 * TOKENS, D), BF)],
        sems=1,
        limit=40,
    )
    recv2 = exchange(send2)
    flipped, packed = call(
        prepare_kernel,
        [((4 * D, D), BF), ((PACKED, D), BF, HERE)],
        (marks, emb, og, halo, decoder_projected, enc_out, dec_qkv, enc_qkv),
        "prepare",
        scratch=[((OWN, D), BF)],
        sems=8,
        limit=40,
    )
    send3, keep, send = call(
        decode_kernel,
        [((GROUPS * 8, 256), BF, HERE), ((4, D, 128), BF), ((4, D, 128), BF)],
        (marks, recv2, flipped, (packed, HERE)),
        "decode",
        scratch=[
            ((GROUPS * 8, 256), BF),
            ((D, D), BF),
            ((D, D), BF),
            ((3 * D, D), BF),
            ((FRAME, D), BF),
            ((3 * D, FRAME), BF),
            ((D, FRAME), BF),
        ],
        sems=5,
        limit=48,
        flops=2 * 10**9,
    )
    recv3 = exchange(send3)
    sums = call(add_kernel, [((D, 128), BF)] * 4, (keep, swap(send, 1)), "add_core")
    parts = [sums[0]] + [swap(sums[j], 2 * j) for j in range(1, 4)]
    (back,) = call(
        encode_back_kernel,
        [((GROUPS * 8, 128), BF)],
        (marks, recv3, (packed, HERE), (kept, HERE)),
        "encode_back",
        scratch=[((D, D), BF), ((4 * TOKENS, D), BF), ((3 * D, D), BF)],
        sems=6,
        limit=48,
        flops=2 * 10**9,
    )
    (send4,) = call(join_kernel, [((GROUPS * 8, 256), BF)], (back, *parts), "join")
    recv4 = exchange(send4)
    tiles, grad_enc, grad_dec = call(
        finish_kernel,
        [((TILE, D), BF), ((8, 64), F32), ((8, 64), F32)],
        (marks, recv4),
        "finish",
    )
    return tiles[None], grad_enc, grad_dec


def solution(mesh):
    placed = (
        P("slide", "grid", None),
        P("slide", None),
        P("slide", None),
        P("slide", "grid", None),
        P(),
        P(),
        P(),
        P(),
        P(),
    )
    return jax.shard_map(
        shards,
        mesh=mesh,
        in_specs=placed,
        out_specs=(P("slide", "grid", None), P("grid", "slide"), P("grid", "slide")),
        check_vma=False,
    )
```

```python
import jax
import jax.numpy as jnp
from jax import lax
from jax.experimental import pallas as pl
from jax.experimental.pallas import tpu as pltpu
from jax.sharding import PartitionSpec as P

HEADS = 8
HEAD = 64
D = 512
TILE = 128
FRAME = 256
RUN = 32
GROUPS = 64
TOKENS = 32
EPS = 1e-06
SCALE = 0.125
LOG2E = 1.4426950408889634
NEG = -1e30
BF = jnp.bfloat16
F32 = jnp.float32
I32 = jnp.int32


def nn(a, b):
    return lax.dot_general(a, b, (((1,), (0,)), ((), ())), preferred_element_type=F32)


def nt(a, b):
    return lax.dot_general(a, b, (((1,), (1,)), ((), ())), preferred_element_type=F32)


def tn(a, b):
    return lax.dot_general(a, b, (((0,), (0,)), ((), ())), preferred_element_type=F32)


def iota(shape, dim):
    return lax.broadcasted_iota(I32, shape, dim)


def onehot(cond):
    return jnp.where(cond, 1.0, 0.0).astype(BF)


class Load:
    def __init__(self, source, held, sems, first, parts=1):
        self.held = held
        rows = held.shape[0] // parts
        spots = [slice(i * rows, (i + 1) * rows) for i in range(parts)]
        self.copies = [
            pltpu.make_async_copy(source.at[spot], held.at[spot], sems.at[first + i]) for i, spot in enumerate(spots)
        ]
        for copy in self.copies:
            copy.start()

    def __call__(self):
        for copy in self.copies:
            copy.wait()
        self.copies = []
        return self.held


def run_counts(visible_ref, limit):
    total = jnp.zeros(limit.shape, I32)
    for q in range(4):
        firsts = visible_ref[:, q * RUN : q * RUN + 1]
        total += jnp.sum(jnp.where(firsts < limit, 1, 0), axis=0, keepdims=True)
    return total


def frame_ranks(visible_ref, first, width):
    lane = iota((1, width), 1)
    limit = first + lane - (lane & (RUN - 1))
    seen = run_counts(visible_ref, limit)
    present = run_counts(visible_ref, limit + RUN) > seen
    return seen * RUN + (lane & (RUN - 1)), present


def own_slots(visible_ref, first):
    rank, present = frame_ranks(visible_ref, first, TILE)
    base = RUN * run_counts(visible_ref, jnp.broadcast_to(first, (1, TILE)))
    return jnp.where(present, (rank & (GROUPS - 1)) * 2 + ((rank - base) >> 6), -1)


def send_tokens_kernel(visible_hbm, emb_hbm, og_hbm, out_hbm, pair_hbm, visible_b, emb_b, og_b, out_ref, sems):
    og = Load(og_hbm, og_b, sems, 2)
    emb = Load(emb_hbm, emb_b, sems, 1)
    visible = Load(visible_hbm, visible_b, sems, 0)
    ship_og = pltpu.make_async_copy(og(), pair_hbm.at[:, D:], sems.at[4])
    ship_og.start()
    emb_ref = emb()
    ship_emb = pltpu.make_async_copy(emb_ref, pair_hbm.at[:, :D], sems.at[3])
    ship_emb.start()
    slot = own_slots(visible(), lax.axis_index("grid") * TILE)
    rows = iota((GROUPS * 8, TILE), 0)
    picks = [onehot(rows == slot * 4 + part) for part in range(4)]
    total = jnp.zeros((GROUPS * 8, TILE), F32)
    for part in range(4):
        total += nn(picks[part], emb_ref[:, part * 128 : (part + 1) * 128])
    out_ref[...] = total.astype(BF)
    ship_out = pltpu.make_async_copy(out_ref, out_hbm, sems.at[5])
    ship_out.start()
    ship_out.wait()
    ship_emb.wait()
    ship_og.wait()


def plan_kernel(visible_ref, wid_ref, enc_qkv_ref, mask_ref, halo_ref, marks_ref, enc_ref):
    enc_ref[...] = enc_qkv_ref[...]
    d = lax.axis_index("grid")
    first = d * TILE
    lane = iota((1, GROUPS * 8), 1)
    peer = lane >> 3
    start1 = RUN * run_counts(visible_ref, peer * TILE)
    stop1 = RUN * run_counts(visible_ref, peer * TILE + TILE)
    low1 = start1 + GROUPS * ((lane >> 2) & 1)
    marks_ref[0:1, :] = low1.astype(F32)
    marks_ref[1:2, :] = jnp.minimum(low1 + GROUPS, stop1).astype(F32)

    wid = wid_ref[...]
    last = wid[:, TILE - 1 :]
    before = jnp.concatenate([jnp.full((1, 1), -1, I32), last[:-1]], axis=0)
    more = jnp.sum(jnp.where(wid == before, 1.0, 0.0), axis=1, keepdims=True).astype(I32)
    head = iota((GROUPS, 1), 0) * TILE + more
    rows = iota((GROUPS, GROUPS * 8), 0)
    begin = jnp.sum(jnp.where(rows == peer, head, 0), axis=0, keepdims=True)
    end = jnp.sum(jnp.where(rows == peer + 1, head, 0), axis=0, keepdims=True)
    end = jnp.where(peer == GROUPS - 1, GROUPS * TILE, end)

    def visible_below(tile):
        total = jnp.zeros(tile.shape, I32)
        for q in range(4):
            firsts = visible_ref[:, q * RUN : q * RUN + 1]
            total += jnp.sum(jnp.clip(tile - firsts, 0, RUN), axis=0, keepdims=True)
        return total

    start2, stop2 = visible_below(begin), visible_below(end)
    low2 = start2 + GROUPS * ((lane >> 1) & 3)
    marks_ref[2:3, :] = low2.astype(F32)
    marks_ref[3:4, :] = jnp.minimum(low2 + GROUPS, stop2).astype(F32)
    marks_ref[4:8, :] = jnp.zeros((4, GROUPS * 8), F32)
    marks_ref[8:16, :] = jnp.broadcast_to(mask_ref[...], (8, D))

    def mine(values):
        return jnp.sum(jnp.where(lane == d * 8, values.astype(F32), 0.0), axis=1, keepdims=True).astype(I32)

    start2, stop2, begin, end = mine(start2), mine(stop2), mine(begin), mine(end)
    rank, present = frame_ranks(visible_ref, first, FRAME)
    spot = iota((1, FRAME), 1)
    live = present & (rank >= start2) & (rank < stop2)
    owned = (first + spot >= begin) & (first + spot < end)
    marks_ref[4:5, :FRAME] = jnp.where(live, (rank & (GROUPS - 1)) * 4 + ((rank - start2) >> 6), -1).astype(F32)
    marks_ref[5:6, :FRAME] = jnp.where(owned, 1.0, 0.0)
    own = wid_ref[pl.ds(d, 1), :]
    after = wid_ref[pl.ds(jnp.minimum(d + 1, GROUPS - 1), 1), :]
    marks_ref[6:7, :FRAME] = jnp.where(owned, jnp.concatenate([own, after], axis=1), -1 - spot).astype(F32)
    marks_ref[7:8, :TILE] = own_slots(visible_ref, first).astype(F32)


OUT_T, BOTH, MORE, OG_ROWS, OWN, QKV, ENC_OUT, ENC_QKV, PACKED = 1536, 0, 512, 1024, 1280, 1280, 2816, 3328, 18432


def blocks(weight_ref, out_ref, first, sems, sem):
    copies = []
    for i in range(weight_ref.shape[1] // D):
        rows = out_ref.at[first + i * D : first + (i + 1) * D]
        copies.append(pltpu.make_async_copy(weight_ref.at[:, i * D : (i + 1) * D], rows, sems.at[sem + i]))
        copies[-1].start()
    return copies


def prepare_kernel(marks_ref, emb_ref, og_ref, halo_ref, proj_ref, enc_out_ref, qkv_ref, enc_qkv_ref, flipped_ref, packed_ref, held, sems):
    copies = blocks(qkv_ref, packed_ref, QKV, sems, 0)
    copies += blocks(enc_out_ref, packed_ref, ENC_OUT, sems, 4) + blocks(enc_qkv_ref, packed_ref, ENC_QKV, sems, 5)
    flipped_ref[:OUT_T, :] = qkv_ref[...].T
    flipped_ref[OUT_T:, :] = enc_out_ref[...].T
    owned = marks_ref[5:6, :FRAME] > 0
    held[OG_ROWS : OG_ROWS + TILE, :] = og_ref[...]
    held[OG_ROWS + TILE : OG_ROWS + FRAME, :] = halo_ref[:, D:]
    og_t = jnp.concatenate([og_ref[...].T, halo_ref[:, D:].T], axis=1).astype(F32)
    og_t = jnp.where(owned, og_t, 0.0).astype(BF)
    held[BOTH:MORE, :FRAME] = nn(proj_ref[...], og_t).astype(BF)
    held[BOTH:MORE, FRAME:] = og_t
    held[MORE : MORE + D, :FRAME] = jnp.concatenate([emb_ref[...].T, halo_ref[:, :D].T], axis=1)
    across = jnp.broadcast_to(marks_ref[6:7, :FRAME], (FRAME, FRAME))
    held[MORE : MORE + FRAME, FRAME:] = jnp.where(across == across.T, 0.0, NEG).astype(BF)
    held[MORE + FRAME : MORE + D, FRAME:] = jnp.zeros((FRAME, FRAME), BF)
    copies.append(pltpu.make_async_copy(held, packed_ref.at[:OWN], sems.at[3]))
    copies[-1].start()
    for copy in copies:
        copy.wait()


def per_head(rows):
    stacked = jnp.concatenate([rows] * HEADS, axis=0)
    shape = stacked.shape
    same = iota(shape, 0) // TOKENS == iota(shape, 1) // HEAD
    return jnp.where(same, stacked.astype(F32), 0.0).astype(BF)


def fold_heads(stacked):
    shape = stacked.shape
    same = iota(shape, 0) // TOKENS == iota(shape, 1) // HEAD
    kept = jnp.where(same, stacked, 0.0)
    total = kept[:TOKENS]
    for h in range(1, HEADS):
        total += kept[h * TOKENS : (h + 1) * TOKENS]
    return total


def group_match(marks_ref, row):
    ranks = iota((TOKENS, GROUPS * 8), 0) * GROUPS + lax.axis_index("grid")
    low, high = marks_ref[row : row + 1, :].astype(I32), marks_ref[row + 1 : row + 2, :].astype(I32)
    return (ranks >= low) & (ranks < high)


def encoder_probs(queries, keys):
    scores = nt(per_head(queries), keys) * SCALE
    weights = jnp.exp(scores - jnp.max(scores, axis=1, keepdims=True))
    return weights / jnp.sum(weights, axis=1, keepdims=True)


def encode_kernel(recv_ref, marks_ref, weight_ref, out_ref, store, kept_ref, sems):
    match1 = group_match(marks_ref, 0)
    lanes = iota((TOKENS, GROUPS * 8), 1)
    recv = recv_ref[...]
    x = jnp.concatenate([nn(onehot(match1 & (lanes % 4 == part)), recv) for part in range(4)], axis=1)
    kept_ref[:TOKENS, :] = x.astype(BF)
    normed = (x * lax.rsqrt(jnp.mean(x * x, axis=1, keepdims=True) + EPS)).astype(BF)
    qkv = nn(normed, weight_ref[...]).astype(BF)
    for i in range(3):
        kept_ref[(i + 1) * TOKENS : (i + 2) * TOKENS, :] = qkv[:, i * D : (i + 1) * D]
    keep = pltpu.make_async_copy(kept_ref, store.at[: 4 * TOKENS], sems.at[0])
    keep.start()
    soft = encoder_probs(qkv[:, :D], qkv[:, D : 2 * D])
    context = fold_heads(nn(soft.astype(BF), qkv[:, 2 * D :])).astype(BF)
    match2 = group_match(marks_ref, 2)
    out = tn(onehot(match2 & (lanes % 2 == 0)), context[:, :256])
    out += tn(onehot(match2 & (lanes % 2 == 1)), context[:, 256:])
    out_ref[...] = out.astype(BF)
    keep.wait()


def decode_kernel(marks_ref, recv_ref, flipped_ref, packed, out_hbm, keep_ref, send_ref, out_ref, more_b, both_b, qkv_b, og_b, dqkv_ref, ctx_ref, sems):
    more = Load(packed.at[MORE:OG_ROWS], more_b, sems, 0)
    both = Load(packed.at[BOTH:MORE], both_b, sems, 1)
    qkv_w = Load(packed.at[QKV : QKV + 3 * D], qkv_b, sems, 2)
    og_rows = Load(packed.at[OG_ROWS:OWN], og_b, sems, 3)
    slot = marks_ref[4:5, :FRAME].astype(I32)
    live = slot >= 0
    owned = marks_ref[5:6, :FRAME] > 0
    blank = jnp.broadcast_to(marks_ref[8:9, :], (TILE, D)).T[:, :1]
    rows = iota((GROUPS * 8, FRAME), 0)
    pick = [onehot(rows == slot * 2 + half) for half in range(2)]
    recv = recv_ref[...]
    ctx_enc = jnp.concatenate([tn(recv, pick[half]) for half in range(2)], axis=0).astype(BF)
    delta = nn(flipped_ref[OUT_T:, :], ctx_enc)
    x = jnp.where(live, (more()[:, :FRAME].astype(F32) + delta).astype(BF).astype(F32), blank)
    inv = lax.rsqrt(jnp.mean(x * x, axis=0, keepdims=True) + EPS)
    normed = (x * inv).astype(BF)
    keys_t = nn(flipped_ref[D : 2 * D, :], normed).astype(BF)
    keys = keys_t.T
    vals_t = nn(flipped_ref[2 * D : OUT_T, :], normed).astype(BF)
    vals = vals_t.T
    qkv = (nn(flipped_ref[:D, :], normed).astype(BF), keys_t, vals_t)
    bias_rows = more()[:FRAME, FRAME:].astype(F32)
    both_b = both()
    for first in range(0, HEADS, 8):
        group = range(first, first + 8)
        q, k, v, d = {}, {}, {}, {}
        for h in group:
            spot = slice(h * HEAD, (h + 1) * HEAD)
            q[h], k[h], v[h] = [block[spot] for block in qkv]
            d[h] = both_b[spot, :FRAME]
        scores = {h: nn(keys[:, h * HEAD : (h + 1) * HEAD], q[h]) for h in group}
        dprobs = {h: nn(vals[:, h * HEAD : (h + 1) * HEAD], d[h]) for h in group}
        probs = {}
        for h in group:
            logits = scores[h] * (SCALE * LOG2E) + bias_rows
            weights = jnp.exp2(logits - jnp.max(logits, axis=0, keepdims=True))
            probs[h] = weights * (1.0 / jnp.sum(weights, axis=0, keepdims=True))
        probs_b = {h: probs[h].astype(BF) for h in group}
        context = {h: nn(v[h], probs_b[h]) for h in group}
        dscores = {}
        for h in group:
            ctx_ref[h * HEAD : (h + 1) * HEAD, :] = jnp.where(owned, context[h], 0.0).astype(BF)
            inner = jnp.sum(context[h] * d[h].astype(F32), axis=0, keepdims=True)
            dscores[h] = (probs[h] * (dprobs[h] - inner)).astype(BF)
        for h in group:
            dqkv_ref[h * HEAD : (h + 1) * HEAD, :] = (nn(k[h], dscores[h]) * SCALE).astype(BF)
            dqkv_ref[D + h * HEAD : D + (h + 1) * HEAD, :] = (nt(q[h], dscores[h]) * SCALE).astype(BF)
            dqkv_ref[2 * D + h * HEAD : 2 * D + (h + 1) * HEAD, :] = nt(d[h], probs_b[h]).astype(BF)

    weight_ref = qkv_w()
    dnormed = nn(weight_ref[:D, :], dqkv_ref[:D, :])
    for i in range(1, 3):
        dnormed += nn(weight_ref[i * D : (i + 1) * D, :], dqkv_ref[i * D : (i + 1) * D, :])
    slope = inv * inv * inv * jnp.mean(x * dnormed, axis=0, keepdims=True)
    dx = (inv * dnormed - x * slope + both_b[:, FRAME:].astype(F32)).astype(BF)
    dx_rows = dx.T
    out = nn(pick[0], dx_rows[:, :256]) + nn(pick[1], dx_rows[:, 256:])
    out_ref[...] = out.astype(BF)
    ship = pltpu.make_async_copy(out_ref, out_hbm, sems.at[4])
    ship.start()

    me = lax.axis_index("slide")
    even = (me & 1) == 0
    grad_enc = nn(ctx_enc, dx_rows).astype(BF)
    grad_dec = nn(ctx_ref[...], og_rows()[...]).astype(BF)

    def block(s):
        spot = slice(s * 64, (s + 1) * 64)
        return jnp.concatenate([grad_enc[:, spot], grad_dec[:, spot]], axis=1)

    for m in range(4):
        low, high = block(2 * m), block(2 * m + 1)
        j = m ^ (me >> 1)
        keep_ref[j] = jnp.where(even, low, high)
        send_ref[j] = jnp.where(even, high, low)
    ship.wait()


def fetch_kernel(packed, enc_out_ref, sems):
    Load(packed.at[ENC_OUT:ENC_QKV], enc_out_ref, sems, 0, 4)()


def add_kernel(keep_ref, recv_ref, fetched, *outs):
    for j in range(4):
        outs[j][...] = (keep_ref[j].astype(F32) + recv_ref[j].astype(F32)).astype(BF)


def encode_back_kernel(marks_ref, recv_ref, enc_out_ref, packed, store, out_ref, kept_b, weight_b, sems):
    kept = Load(store.at[: 4 * TOKENS], kept_b, sems, 0)
    weight = Load(packed.at[ENC_QKV : ENC_QKV + 3 * D], weight_b, sems, 1, 3)
    match2 = group_match(marks_ref, 2)
    lanes = iota((TOKENS, GROUPS * 8), 1)
    recv = recv_ref[...]
    grad = jnp.concatenate(
        [nn(onehot(match2 & (lanes % 2 == half)), recv) for half in range(2)], axis=1
    )
    dctx = per_head(nt(grad.astype(BF), enc_out_ref[...]).astype(BF))
    kept_ref = kept()
    queries, keys, values = [kept_ref[i * TOKENS : (i + 1) * TOKENS, :] for i in range(1, 4)]
    probs = encoder_probs(queries, keys)
    dprobs = nt(dctx, values).astype(BF).astype(F32)
    inner = jnp.sum(probs * dprobs, axis=1, keepdims=True)
    dscores = (probs * (dprobs - inner) * SCALE).astype(BF)
    dq = fold_heads(nn(dscores, keys))
    dk = tn(dscores, per_head(queries))
    dv = tn(probs.astype(BF), dctx)
    weight_ref = weight()
    dnormed = nt(dq.astype(BF), weight_ref[:D, :])
    dnormed += nt(dk.astype(BF), weight_ref[D : 2 * D, :])
    dnormed += nt(dv.astype(BF), weight_ref[2 * D :, :])
    dnormed = dnormed.astype(BF).astype(F32)
    x = kept_ref[:TOKENS, :].astype(F32)
    inv = lax.rsqrt(jnp.mean(x * x, axis=1, keepdims=True) + EPS)
    slope = inv * inv * inv * jnp.mean(x * dnormed, axis=1, keepdims=True)
    dtokens = (grad + (inv * dnormed - x * slope)).astype(BF)
    match1 = group_match(marks_ref, 0)
    out = jnp.zeros((GROUPS * 8, 128), F32)
    for part in range(4):
        out += tn(onehot(match1 & (lanes % 4 == part)), dtokens[:, part * 128 : (part + 1) * 128])
    out_ref[...] = out.astype(BF)


def join_kernel(tokens_ref, part0, part1, part2, part3, out_ref):
    out_ref[:, :128] = tokens_ref[...]
    parts = [p[...].astype(F32) for p in (part0, part1, part2, part3)]
    out_ref[:, 128:] = (parts[0] + parts[1] + parts[2] + parts[3]).astype(BF)


def finish_kernel(marks_ref, recv_ref, tiles_ref, enc_ref, dec_ref):
    slot = jnp.broadcast_to(marks_ref[7:8, :TILE], (TILE, TILE)).T[:, 0:1].astype(I32)
    lanes = iota((TILE, GROUPS * 8), 1)
    recv = recv_ref[:, :128]
    for part in range(4):
        tiles_ref[:, part * 128 : (part + 1) * 128] = nn(onehot(lanes == slot * 4 + part), recv).astype(BF)
    rows = recv_ref[:, 128:].astype(F32).reshape(GROUPS, 8, 128)
    total = jnp.sum(rows, axis=0)
    enc_ref[...] = total[:, :64]
    dec_ref[...] = total[:, 64:]


VM = pl.BlockSpec(memory_space=pltpu.VMEM)
HERE = pl.BlockSpec(memory_space=pl.ANY)


def call(kernel, outs, args, name, scratch=(), limit=16, flops=10**8, sems=0):
    ins = [a if isinstance(a, tuple) else (a, VM) for a in args]
    held = [pltpu.VMEM(shape, dtype) for shape, dtype in scratch]
    return pl.pallas_call(
        kernel,
        out_shape=[jax.ShapeDtypeStruct(o[0], o[1]) for o in outs],
        in_specs=[place for _, place in ins],
        out_specs=[o[2] if len(o) > 2 else VM for o in outs],
        scratch_shapes=held + ([pltpu.SemaphoreType.DMA((sems,))] if sems else []),
        compiler_params=pltpu.CompilerParams(vmem_limit_bytes=limit * 1024 * 1024),
        cost_estimate=pl.CostEstimate(flops=flops, bytes_accessed=2 * 10**6, transcendentals=0),
        name=name,
    )(*[a for a, _ in ins])


def exchange(rows):
    return lax.all_to_all(rows, "grid", split_axis=0, concat_axis=0, tiled=True)


def swap(block, bit):
    return lax.ppermute(block, "slide", [(i, i ^ bit) for i in range(8)])


def shards(
    embeddings,
    visible,
    window_id,
    output_gradient,
    mask_token,
    enc_qkv,
    enc_out,
    dec_qkv,
    decoder_projected,
):
    emb = embeddings[0]
    og = output_gradient[0]
    ranks = visible.reshape(16, 128)
    send1, pair = call(
        send_tokens_kernel,
        [((GROUPS * 8, 128), BF, HERE), ((TILE, 2 * D), BF, HERE)],
        ((ranks, HERE), (emb, HERE), (og, HERE)),
        "send_tokens",
        scratch=[((16, 128), I32), ((TILE, D), BF), ((TILE, D), BF), ((GROUPS * 8, 128), BF)],
        sems=6,
        limit=62,
    )
    halo = lax.ppermute(pair, "grid", [(i + 1, i) for i in range(GROUPS - 1)])
    recv1 = exchange(send1)
    marks, enc = call(
        plan_kernel,
        [((16, GROUPS * 8), F32), ((D, 3 * D), BF)],
        (ranks, window_id.reshape(GROUPS, TILE), enc_qkv, mask_token[None, :], (halo, HERE)),
        "plan",
        flops=4 * 10**9,
    )
    send2, kept = call(
        encode_kernel,
        [((GROUPS * 8, 256), BF), ((PACKED, D), BF, HERE)],
        (recv1, marks, enc),
        "encode",
        scratch=[((4 * TOKENS, D), BF)],
        sems=1,
        limit=40,
    )
    recv2 = exchange(send2)
    flipped, packed = call(
        prepare_kernel,
        [((4 * D, D), BF), ((PACKED, D), BF, HERE)],
        (marks, emb, og, halo, decoder_projected, enc_out, dec_qkv, enc_qkv),
        "prepare",
        scratch=[((OWN, D), BF)],
        sems=8,
        limit=40,
    )
    send3, keep, send = call(
        decode_kernel,
        [((GROUPS * 8, 256), BF, HERE), ((4, D, 128), BF), ((4, D, 128), BF)],
        (marks, recv2, flipped, (packed, HERE)),
        "decode",
        scratch=[
            ((GROUPS * 8, 256), BF),
            ((D, D), BF),
            ((D, D), BF),
            ((3 * D, D), BF),
            ((FRAME, D), BF),
            ((3 * D, FRAME), BF),
            ((D, FRAME), BF),
        ],
        sems=5,
        limit=48,
        flops=2 * 10**9,
    )
    recv3 = exchange(send3)
    part = swap(send, 1)
    (enc_out_b,) = call(fetch_kernel, [((D, D), BF)], ((packed, HERE),), "fetch", sems=4, limit=40)
    sums = call(add_kernel, [((D, 128), BF)] * 4, (keep, part, (enc_out_b, HERE)), "add_core")
    parts = [sums[0]] + [swap(sums[j], 2 * j) for j in (2, 1, 3)]
    (back,) = call(
        encode_back_kernel,
        [((GROUPS * 8, 128), BF)],
        (marks, recv3, enc_out_b, (packed, HERE), (kept, HERE)),
        "encode_back",
        scratch=[((4 * TOKENS, D), BF), ((3 * D, D), BF)],
        sems=4,
        limit=48,
        flops=2 * 10**9,
    )
    (send4,) = call(join_kernel, [((GROUPS * 8, 256), BF)], (back, *parts), "join")
    recv4 = exchange(send4)
    tiles, grad_enc, grad_dec = call(
        finish_kernel,
        [((TILE, D), BF), ((8, 64), F32), ((8, 64), F32)],
        (marks, recv4),
        "finish",
    )
    return tiles[None], grad_enc, grad_dec


def solution(mesh):
    placed = (
        P("slide", "grid", None),
        P("slide", None),
        P("slide", None),
        P("slide", "grid", None),
        P(),
        P(),
        P(),
        P(),
        P(),
    )
    return jax.shard_map(
        shards,
        mesh=mesh,
        in_specs=placed,
        out_specs=(P("slide", "grid", None), P("grid", "slide"), P("grid", "slide")),
        check_vma=False,
    )
```

```python
import jax
import jax.numpy as jnp
from jax import lax
from jax.experimental import pallas as pl
from jax.experimental.pallas import tpu as pltpu
from jax.sharding import PartitionSpec as P

HEADS = 8
HEAD = 64
D = 512
TILE = 128
FRAME = 256
RUN = 32
GROUPS = 64
TOKENS = 32
EPS = 1e-06
SCALE = 0.125
LOG2E = 1.4426950408889634
NEG = -1e30
BF = jnp.bfloat16
F32 = jnp.float32
I32 = jnp.int32


def nn(a, b):
    return lax.dot_general(a, b, (((1,), (0,)), ((), ())), preferred_element_type=F32)


def nt(a, b):
    return lax.dot_general(a, b, (((1,), (1,)), ((), ())), preferred_element_type=F32)


def tn(a, b):
    return lax.dot_general(a, b, (((0,), (0,)), ((), ())), preferred_element_type=F32)


def iota(shape, dim):
    return lax.broadcasted_iota(I32, shape, dim)


def onehot(cond):
    return jnp.where(cond, 1.0, 0.0).astype(BF)


class Load:
    def __init__(self, source, held, sems, first, parts=1):
        self.held = held
        rows = held.shape[0] // parts
        spots = [slice(i * rows, (i + 1) * rows) for i in range(parts)]
        self.copies = [
            pltpu.make_async_copy(source.at[spot], held.at[spot], sems.at[first + i]) for i, spot in enumerate(spots)
        ]
        for copy in self.copies:
            copy.start()

    def __call__(self):
        for copy in self.copies:
            copy.wait()
        self.copies = []
        return self.held


def run_counts(visible_ref, limit):
    total = jnp.zeros(limit.shape, I32)
    for q in range(4):
        firsts = visible_ref[:, q * RUN : q * RUN + 1]
        total += jnp.sum(jnp.where(firsts < limit, 1, 0), axis=0, keepdims=True)
    return total


def frame_ranks(visible_ref, first, width):
    lane = iota((1, width), 1)
    limit = first + lane - (lane & (RUN - 1))
    seen = run_counts(visible_ref, limit)
    present = run_counts(visible_ref, limit + RUN) > seen
    return seen * RUN + (lane & (RUN - 1)), present


def own_slots(visible_ref, first):
    rank, present = frame_ranks(visible_ref, first, TILE)
    base = RUN * run_counts(visible_ref, jnp.broadcast_to(first, (1, TILE)))
    return jnp.where(present, (rank & (GROUPS - 1)) * 2 + ((rank - base) >> 6), -1)


def send_tokens_kernel(visible_hbm, emb_hbm, og_hbm, out_hbm, pair_hbm, visible_b, emb_b, og_b, out_ref, sems):
    og = Load(og_hbm, og_b, sems, 2)
    emb = Load(emb_hbm, emb_b, sems, 1)
    visible = Load(visible_hbm, visible_b, sems, 0)
    ship_og = pltpu.make_async_copy(og(), pair_hbm.at[:, D:], sems.at[4])
    ship_og.start()
    emb_ref = emb()
    ship_emb = pltpu.make_async_copy(emb_ref, pair_hbm.at[:, :D], sems.at[3])
    ship_emb.start()
    slot = own_slots(visible(), lax.axis_index("grid") * TILE)
    rows = iota((GROUPS * 8, TILE), 0)
    picks = [onehot(rows == slot * 4 + part) for part in range(4)]
    total = jnp.zeros((GROUPS * 8, TILE), F32)
    for part in range(4):
        total += nn(picks[part], emb_ref[:, part * 128 : (part + 1) * 128])
    out_ref[...] = total.astype(BF)
    ship_out = pltpu.make_async_copy(out_ref, out_hbm, sems.at[5])
    ship_out.start()
    ship_out.wait()
    ship_emb.wait()
    ship_og.wait()


def plan_kernel(visible_ref, wid_ref, enc_qkv_ref, mask_ref, halo_ref, marks_ref, enc_ref):
    enc_ref[...] = enc_qkv_ref[...]
    d = lax.axis_index("grid")
    first = d * TILE
    lane = iota((1, GROUPS * 8), 1)
    peer = lane >> 3
    start1 = RUN * run_counts(visible_ref, peer * TILE)
    stop1 = RUN * run_counts(visible_ref, peer * TILE + TILE)
    low1 = start1 + GROUPS * ((lane >> 2) & 1)
    marks_ref[0:1, :] = low1.astype(F32)
    marks_ref[1:2, :] = jnp.minimum(low1 + GROUPS, stop1).astype(F32)

    wid = wid_ref[...]
    last = wid[:, TILE - 1 :]
    before = jnp.concatenate([jnp.full((1, 1), -1, I32), last[:-1]], axis=0)
    more = jnp.sum(jnp.where(wid == before, 1.0, 0.0), axis=1, keepdims=True).astype(I32)
    head = iota((GROUPS, 1), 0) * TILE + more
    rows = iota((GROUPS, GROUPS * 8), 0)
    begin = jnp.sum(jnp.where(rows == peer, head, 0), axis=0, keepdims=True)
    end = jnp.sum(jnp.where(rows == peer + 1, head, 0), axis=0, keepdims=True)
    end = jnp.where(peer == GROUPS - 1, GROUPS * TILE, end)

    def visible_below(tile):
        total = jnp.zeros(tile.shape, I32)
        for q in range(4):
            firsts = visible_ref[:, q * RUN : q * RUN + 1]
            total += jnp.sum(jnp.clip(tile - firsts, 0, RUN), axis=0, keepdims=True)
        return total

    start2, stop2 = visible_below(begin), visible_below(end)
    low2 = start2 + GROUPS * ((lane >> 1) & 3)
    marks_ref[2:3, :] = low2.astype(F32)
    marks_ref[3:4, :] = jnp.minimum(low2 + GROUPS, stop2).astype(F32)
    marks_ref[4:8, :] = jnp.zeros((4, GROUPS * 8), F32)
    marks_ref[8:16, :] = jnp.broadcast_to(mask_ref[...], (8, D))

    def mine(values):
        return jnp.sum(jnp.where(lane == d * 8, values.astype(F32), 0.0), axis=1, keepdims=True).astype(I32)

    start2, stop2, begin, end = mine(start2), mine(stop2), mine(begin), mine(end)
    rank, present = frame_ranks(visible_ref, first, FRAME)
    spot = iota((1, FRAME), 1)
    live = present & (rank >= start2) & (rank < stop2)
    owned = (first + spot >= begin) & (first + spot < end)
    marks_ref[4:5, :FRAME] = jnp.where(live, (rank & (GROUPS - 1)) * 4 + ((rank - start2) >> 6), -1).astype(F32)
    marks_ref[5:6, :FRAME] = jnp.where(owned, 1.0, 0.0)
    own = wid_ref[pl.ds(d, 1), :]
    after = wid_ref[pl.ds(jnp.minimum(d + 1, GROUPS - 1), 1), :]
    marks_ref[6:7, :FRAME] = jnp.where(owned, jnp.concatenate([own, after], axis=1), -1 - spot).astype(F32)
    marks_ref[7:8, :TILE] = own_slots(visible_ref, first).astype(F32)


OUT_T, BOTH, MORE, OG_ROWS, OWN, QKV, ENC_OUT, ENC_QKV, PACKED = 1536, 0, 512, 1024, 1280, 1280, 2816, 3328, 18432


def blocks(weight_ref, out_ref, first, sems, sem):
    copies = []
    for i in range(weight_ref.shape[1] // D):
        rows = out_ref.at[first + i * D : first + (i + 1) * D]
        copies.append(pltpu.make_async_copy(weight_ref.at[:, i * D : (i + 1) * D], rows, sems.at[sem + i]))
        copies[-1].start()
    return copies


def prepare_kernel(marks_ref, emb_ref, og_ref, halo_ref, proj_ref, enc_out_ref, qkv_ref, enc_qkv_ref, flipped_ref, packed_ref, held, sems):
    copies = blocks(qkv_ref, packed_ref, QKV, sems, 0)
    copies += blocks(enc_out_ref, packed_ref, ENC_OUT, sems, 4) + blocks(enc_qkv_ref, packed_ref, ENC_QKV, sems, 5)
    flipped_ref[:OUT_T, :] = qkv_ref[...].T
    flipped_ref[OUT_T:, :] = enc_out_ref[...].T
    owned = marks_ref[5:6, :FRAME] > 0
    held[OG_ROWS : OG_ROWS + TILE, :] = og_ref[...]
    held[OG_ROWS + TILE : OG_ROWS + FRAME, :] = halo_ref[:, D:]
    og_t = jnp.concatenate([og_ref[...].T, halo_ref[:, D:].T], axis=1).astype(F32)
    og_t = jnp.where(owned, og_t, 0.0).astype(BF)
    held[BOTH:MORE, :FRAME] = nn(proj_ref[...], og_t).astype(BF)
    held[BOTH:MORE, FRAME:] = og_t
    held[MORE : MORE + D, :FRAME] = jnp.concatenate([emb_ref[...].T, halo_ref[:, :D].T], axis=1)
    across = jnp.broadcast_to(marks_ref[6:7, :FRAME], (FRAME, FRAME))
    held[MORE : MORE + FRAME, FRAME:] = jnp.where(across == across.T, 0.0, NEG).astype(BF)
    held[MORE + FRAME : MORE + D, FRAME:] = jnp.zeros((FRAME, FRAME), BF)
    copies.append(pltpu.make_async_copy(held, packed_ref.at[:OWN], sems.at[3]))
    copies[-1].start()
    for copy in copies:
        copy.wait()


def per_head(rows):
    stacked = jnp.concatenate([rows] * HEADS, axis=0)
    shape = stacked.shape
    same = iota(shape, 0) // TOKENS == iota(shape, 1) // HEAD
    return jnp.where(same, stacked.astype(F32), 0.0).astype(BF)


def fold_heads(stacked):
    shape = stacked.shape
    same = iota(shape, 0) // TOKENS == iota(shape, 1) // HEAD
    kept = jnp.where(same, stacked, 0.0)
    total = kept[:TOKENS]
    for h in range(1, HEADS):
        total += kept[h * TOKENS : (h + 1) * TOKENS]
    return total


def group_match(marks_ref, row):
    ranks = iota((TOKENS, GROUPS * 8), 0) * GROUPS + lax.axis_index("grid")
    low, high = marks_ref[row : row + 1, :].astype(I32), marks_ref[row + 1 : row + 2, :].astype(I32)
    return (ranks >= low) & (ranks < high)


def encoder_probs(queries, keys):
    scores = nt(per_head(queries), keys) * SCALE
    weights = jnp.exp(scores - jnp.max(scores, axis=1, keepdims=True))
    return weights / jnp.sum(weights, axis=1, keepdims=True)


def encode_kernel(recv_ref, marks_ref, weight_ref, out_ref, store, kept_ref, sems):
    match1 = group_match(marks_ref, 0)
    lanes = iota((TOKENS, GROUPS * 8), 1)
    recv = recv_ref[...]
    x = jnp.concatenate([nn(onehot(match1 & (lanes % 4 == part)), recv) for part in range(4)], axis=1)
    kept_ref[:TOKENS, :] = x.astype(BF)
    normed = (x * lax.rsqrt(jnp.mean(x * x, axis=1, keepdims=True) + EPS)).astype(BF)
    qkv = nn(normed, weight_ref[...]).astype(BF)
    for i in range(3):
        kept_ref[(i + 1) * TOKENS : (i + 2) * TOKENS, :] = qkv[:, i * D : (i + 1) * D]
    keep = pltpu.make_async_copy(kept_ref, store.at[: 4 * TOKENS], sems.at[0])
    keep.start()
    soft = encoder_probs(qkv[:, :D], qkv[:, D : 2 * D])
    context = fold_heads(nn(soft.astype(BF), qkv[:, 2 * D :])).astype(BF)
    match2 = group_match(marks_ref, 2)
    out = tn(onehot(match2 & (lanes % 2 == 0)), context[:, :256])
    out += tn(onehot(match2 & (lanes % 2 == 1)), context[:, 256:])
    out_ref[...] = out.astype(BF)
    keep.wait()


def decode_kernel(marks_ref, recv_ref, flipped_ref, packed, out_hbm, keep_ref, send_ref, out_ref, more_b, both_b, qkv_b, og_b, dqkv_ref, ctx_ref, sems):
    more = Load(packed.at[MORE:OG_ROWS], more_b, sems, 0)
    both = Load(packed.at[BOTH:MORE], both_b, sems, 1)
    qkv_w = Load(packed.at[QKV : QKV + 3 * D], qkv_b, sems, 2)
    og_rows = Load(packed.at[OG_ROWS:OWN], og_b, sems, 3)
    slot = marks_ref[4:5, :FRAME].astype(I32)
    live = slot >= 0
    owned = marks_ref[5:6, :FRAME] > 0
    blank = jnp.broadcast_to(marks_ref[8:9, :], (TILE, D)).T[:, :1]
    rows = iota((GROUPS * 8, FRAME), 0)
    pick = [onehot(rows == slot * 2 + half) for half in range(2)]
    recv = recv_ref[...]
    ctx_enc = jnp.concatenate([tn(recv, pick[half]) for half in range(2)], axis=0).astype(BF)
    delta = nn(flipped_ref[OUT_T:, :], ctx_enc)
    x = jnp.where(live, (more()[:, :FRAME].astype(F32) + delta).astype(BF).astype(F32), blank)
    inv = lax.rsqrt(jnp.mean(x * x, axis=0, keepdims=True) + EPS)
    normed = (x * inv).astype(BF)
    keys_t = nn(flipped_ref[D : 2 * D, :], normed).astype(BF)
    keys = keys_t.T
    vals_t = nn(flipped_ref[2 * D : OUT_T, :], normed).astype(BF)
    vals = vals_t.T
    qkv = (nn(flipped_ref[:D, :], normed).astype(BF), keys_t, vals_t)
    bias_rows = more()[:FRAME, FRAME:].astype(F32)
    both_b = both()
    for first in range(0, HEADS, 8):
        group = range(first, first + 8)
        q, k, v, d = {}, {}, {}, {}
        for h in group:
            spot = slice(h * HEAD, (h + 1) * HEAD)
            q[h], k[h], v[h] = [block[spot] for block in qkv]
            d[h] = both_b[spot, :FRAME]
        scores = {h: nn(keys[:, h * HEAD : (h + 1) * HEAD], q[h]) for h in group}
        dprobs = {h: nn(vals[:, h * HEAD : (h + 1) * HEAD], d[h]) for h in group}
        probs = {}
        for h in group:
            logits = scores[h] * (SCALE * LOG2E) + bias_rows
            weights = jnp.exp2(logits - jnp.max(logits, axis=0, keepdims=True))
            probs[h] = weights * (1.0 / jnp.sum(weights, axis=0, keepdims=True))
        probs_b = {h: probs[h].astype(BF) for h in group}
        context = {h: nn(v[h], probs_b[h]) for h in group}
        dscores = {}
        for h in group:
            ctx_ref[h * HEAD : (h + 1) * HEAD, :] = jnp.where(owned, context[h], 0.0).astype(BF)
            inner = jnp.sum(context[h] * d[h].astype(F32), axis=0, keepdims=True)
            dscores[h] = (probs[h] * (dprobs[h] - inner)).astype(BF)
        for h in group:
            dqkv_ref[h * HEAD : (h + 1) * HEAD, :] = (nn(k[h], dscores[h]) * SCALE).astype(BF)
            dqkv_ref[D + h * HEAD : D + (h + 1) * HEAD, :] = (nt(q[h], dscores[h]) * SCALE).astype(BF)
            dqkv_ref[2 * D + h * HEAD : 2 * D + (h + 1) * HEAD, :] = nt(d[h], probs_b[h]).astype(BF)

    weight_ref = qkv_w()
    dnormed = nn(weight_ref[:D, :], dqkv_ref[:D, :])
    for i in range(1, 3):
        dnormed += nn(weight_ref[i * D : (i + 1) * D, :], dqkv_ref[i * D : (i + 1) * D, :])
    slope = inv * inv * inv * jnp.mean(x * dnormed, axis=0, keepdims=True)
    dx = (inv * dnormed - x * slope + both_b[:, FRAME:].astype(F32)).astype(BF)
    dx_rows = dx.T
    out = nn(pick[0], dx_rows[:, :256]) + nn(pick[1], dx_rows[:, 256:])
    out_ref[...] = out.astype(BF)
    ship = pltpu.make_async_copy(out_ref, out_hbm, sems.at[4])
    ship.start()

    me = lax.axis_index("slide")
    even = (me & 1) == 0
    grad_enc = nn(ctx_enc, dx_rows).astype(BF)
    grad_dec = nn(ctx_ref[...], og_rows()[...]).astype(BF)

    def block(s):
        spot = slice(s * 64, (s + 1) * 64)
        return jnp.concatenate([grad_enc[:, spot], grad_dec[:, spot]], axis=1)

    for m in range(4):
        low, high = block(2 * m), block(2 * m + 1)
        j = m ^ (me >> 1)
        keep_ref[j] = jnp.where(even, low, high)
        send_ref[j] = jnp.where(even, high, low)
    ship.wait()


def fetch_kernel(packed, first_ref, sems):
    Load(packed.at[ENC_OUT : ENC_QKV + D], first_ref, sems, 0, 4)()


def add_kernel(keep_ref, recv_ref, fetched, *outs):
    for j in range(4):
        outs[j][...] = (keep_ref[j].astype(F32) + recv_ref[j].astype(F32)).astype(BF)


def encode_back_kernel(marks_ref, recv_ref, first_ref, packed, store, out_ref, kept_b, weight_b, sems):
    kept = Load(store.at[: 4 * TOKENS], kept_b, sems, 0)
    weight = Load(packed.at[ENC_QKV + D : ENC_QKV + 3 * D], weight_b, sems, 1, 2)
    match2 = group_match(marks_ref, 2)
    lanes = iota((TOKENS, GROUPS * 8), 1)
    recv = recv_ref[...]
    grad = jnp.concatenate(
        [nn(onehot(match2 & (lanes % 2 == half)), recv) for half in range(2)], axis=1
    )
    dctx = per_head(nt(grad.astype(BF), first_ref[:D, :]).astype(BF))
    kept_ref = kept()
    queries, keys, values = [kept_ref[i * TOKENS : (i + 1) * TOKENS, :] for i in range(1, 4)]
    probs = encoder_probs(queries, keys)
    dprobs = nt(dctx, values).astype(BF).astype(F32)
    inner = jnp.sum(probs * dprobs, axis=1, keepdims=True)
    dscores = (probs * (dprobs - inner) * SCALE).astype(BF)
    dq = fold_heads(nn(dscores, keys))
    dk = tn(dscores, per_head(queries))
    dv = tn(probs.astype(BF), dctx)
    dnormed = nt(dq.astype(BF), first_ref[D:, :])
    weight_ref = weight()
    dnormed += nt(dk.astype(BF), weight_ref[:D, :])
    dnormed += nt(dv.astype(BF), weight_ref[D:, :])
    dnormed = dnormed.astype(BF).astype(F32)
    x = kept_ref[:TOKENS, :].astype(F32)
    inv = lax.rsqrt(jnp.mean(x * x, axis=1, keepdims=True) + EPS)
    slope = inv * inv * inv * jnp.mean(x * dnormed, axis=1, keepdims=True)
    dtokens = (grad + (inv * dnormed - x * slope)).astype(BF)
    match1 = group_match(marks_ref, 0)
    out = jnp.zeros((GROUPS * 8, 128), F32)
    for part in range(4):
        out += tn(onehot(match1 & (lanes % 4 == part)), dtokens[:, part * 128 : (part + 1) * 128])
    out_ref[...] = out.astype(BF)


def join_kernel(tokens_ref, part0, part1, part2, part3, out_ref):
    out_ref[:, :128] = tokens_ref[...]
    parts = [p[...].astype(F32) for p in (part0, part1, part2, part3)]
    out_ref[:, 128:] = (parts[0] + parts[1] + parts[2] + parts[3]).astype(BF)


def finish_kernel(marks_ref, recv_ref, tiles_ref, enc_ref, dec_ref):
    slot = jnp.broadcast_to(marks_ref[7:8, :TILE], (TILE, TILE)).T[:, 0:1].astype(I32)
    lanes = iota((TILE, GROUPS * 8), 1)
    recv = recv_ref[:, :128]
    for part in range(4):
        tiles_ref[:, part * 128 : (part + 1) * 128] = nn(onehot(lanes == slot * 4 + part), recv).astype(BF)
    rows = recv_ref[:, 128:].astype(F32).reshape(GROUPS, 8, 128)
    total = jnp.sum(rows, axis=0)
    enc_ref[...] = total[:, :64]
    dec_ref[...] = total[:, 64:]


VM = pl.BlockSpec(memory_space=pltpu.VMEM)
HERE = pl.BlockSpec(memory_space=pl.ANY)


def call(kernel, outs, args, name, scratch=(), limit=16, flops=10**8, sems=0):
    ins = [a if isinstance(a, tuple) else (a, VM) for a in args]
    held = [pltpu.VMEM(shape, dtype) for shape, dtype in scratch]
    return pl.pallas_call(
        kernel,
        out_shape=[jax.ShapeDtypeStruct(o[0], o[1]) for o in outs],
        in_specs=[place for _, place in ins],
        out_specs=[o[2] if len(o) > 2 else VM for o in outs],
        scratch_shapes=held + ([pltpu.SemaphoreType.DMA((sems,))] if sems else []),
        compiler_params=pltpu.CompilerParams(vmem_limit_bytes=limit * 1024 * 1024),
        cost_estimate=pl.CostEstimate(flops=flops, bytes_accessed=2 * 10**6, transcendentals=0),
        name=name,
    )(*[a for a, _ in ins])


def exchange(rows):
    return lax.all_to_all(rows, "grid", split_axis=0, concat_axis=0, tiled=True)


def swap(block, bit):
    return lax.ppermute(block, "slide", [(i, i ^ bit) for i in range(8)])


def shards(
    embeddings,
    visible,
    window_id,
    output_gradient,
    mask_token,
    enc_qkv,
    enc_out,
    dec_qkv,
    decoder_projected,
):
    emb = embeddings[0]
    og = output_gradient[0]
    ranks = visible.reshape(16, 128)
    send1, pair = call(
        send_tokens_kernel,
        [((GROUPS * 8, 128), BF, HERE), ((TILE, 2 * D), BF, HERE)],
        ((ranks, HERE), (emb, HERE), (og, HERE)),
        "send_tokens",
        scratch=[((16, 128), I32), ((TILE, D), BF), ((TILE, D), BF), ((GROUPS * 8, 128), BF)],
        sems=6,
        limit=62,
    )
    halo = lax.ppermute(pair, "grid", [(i + 1, i) for i in range(GROUPS - 1)])
    recv1 = exchange(send1)
    marks, enc = call(
        plan_kernel,
        [((16, GROUPS * 8), F32), ((D, 3 * D), BF)],
        (ranks, window_id.reshape(GROUPS, TILE), enc_qkv, mask_token[None, :], (halo, HERE)),
        "plan",
        flops=4 * 10**9,
    )
    send2, kept = call(
        encode_kernel,
        [((GROUPS * 8, 256), BF), ((PACKED, D), BF, HERE)],
        (recv1, marks, enc),
        "encode",
        scratch=[((4 * TOKENS, D), BF)],
        sems=1,
        limit=40,
    )
    recv2 = exchange(send2)
    flipped, packed = call(
        prepare_kernel,
        [((4 * D, D), BF), ((PACKED, D), BF, HERE)],
        (marks, emb, og, halo, decoder_projected, enc_out, dec_qkv, enc_qkv),
        "prepare",
        scratch=[((OWN, D), BF)],
        sems=8,
        limit=40,
    )
    send3, keep, send = call(
        decode_kernel,
        [((GROUPS * 8, 256), BF, HERE), ((4, D, 128), BF), ((4, D, 128), BF)],
        (marks, recv2, flipped, (packed, HERE)),
        "decode",
        scratch=[
            ((GROUPS * 8, 256), BF),
            ((D, D), BF),
            ((D, D), BF),
            ((3 * D, D), BF),
            ((FRAME, D), BF),
            ((3 * D, FRAME), BF),
            ((D, FRAME), BF),
        ],
        sems=5,
        limit=48,
        flops=2 * 10**9,
    )
    recv3 = exchange(send3)
    part = swap(send, 1)
    (first_b,) = call(fetch_kernel, [((2 * D, D), BF)], ((packed, HERE),), "fetch", sems=4, limit=40)
    sums = call(add_kernel, [((D, 128), BF)] * 4, (keep, part, (first_b, HERE)), "add_core")
    parts = [sums[0]] + [swap(sums[j], 2 * j) for j in (2, 1, 3)]
    (back,) = call(
        encode_back_kernel,
        [((GROUPS * 8, 128), BF)],
        (marks, recv3, first_b, (packed, HERE), (kept, HERE)),
        "encode_back",
        scratch=[((4 * TOKENS, D), BF), ((2 * D, D), BF)],
        sems=3,
        limit=48,
        flops=2 * 10**9,
    )
    (send4,) = call(join_kernel, [((GROUPS * 8, 256), BF)], (back, *parts), "join")
    recv4 = exchange(send4)
    tiles, grad_enc, grad_dec = call(
        finish_kernel,
        [((TILE, D), BF), ((8, 64), F32), ((8, 64), F32)],
        (marks, recv4),
        "finish",
    )
    return tiles[None], grad_enc, grad_dec


def solution(mesh):
    placed = (
        P("slide", "grid", None),
        P("slide", None),
        P("slide", None),
        P("slide", "grid", None),
        P(),
        P(),
        P(),
        P(),
        P(),
    )
    return jax.shard_map(
        shards,
        mesh=mesh,
        in_specs=placed,
        out_specs=(P("slide", "grid", None), P("grid", "slide"), P("grid", "slide")),
        check_vma=False,
    )
```
